32 devices in a mesh: grp: 2 (over y), path: 16 (over z, x, core).
Axes of the slice: x: 2, y: 2, z: 4, core: 2. Of those that a mesh axis runs over, the one named last changes fastest.
Arguments:
- start_state: float32 [100, 4096], P(None, 'path'), may hold values from -6 to 6
- shocks: float32 [100, 4096], P(None, 'path'), may hold values from -6 to 6
- drift_rate: float32 [100], replicated, may hold values from -0.5 to 0.5
- vol_curve: float32 [100], replicated, may hold values from 0.2 to 1
- weight_in: float32 [2, 1024, 100], P('grp'), may hold values from -0.625 to 0.625
- bias_in: float32 [2, 1024], P('grp'), may hold values from -3 to 3
- weight_out: float32 [2, 1024], P('grp'), may hold values from -0.1875 to 0.1875
- default_date: int32 [4096], P('path'), may hold values from 1 to 3
- netting_set: int32 [4096], P('path'), may hold values from 0 to 15
- loss_given: float32 [16], replicated, may hold values from 0.3 to 0.9
Outputs:
- residual: float32 [2, 4096], P('grp', 'path')
- step_weight_in: float32 [2, 1024, 100], P('grp')
- step_bias: float32 [2, 1024], P('grp')
- step_weight_out: float32 [2, 1024], P('grp')
- curve_step: float32 [2, 100], replicated
The draws below stay inside these ranges and needn't reach their ends.
All inputs are finite; a program needn't handle non-finite values.
Results may differ from the reference program's by a relative error of at most 0.0003.
Values sent between devices are 32-bit elements; how exact they have to be, the bound alone decides.
A program may use at most 64 MiB of HBM per device.

```python
import math
import jax
import jax.numpy as jnp
from jax import lax

F = 100
H = 1024
S = 16
NP = 4096


def touch_ends(result, rng, low, high):
    spot = [jax.random.randint(jax.random.fold_in(rng, axis), (), 0, length) for axis, length in enumerate(result.shape)]
    widest = result.shape.index(max(result.shape))
    neighbour = spot[:widest] + [(spot[widest] + 1) % result.shape[widest]] + spot[widest + 1:]
    return result.at[tuple(spot)].set(low).at[tuple(neighbour)].set(high)


def block_scale(key, shape, cuts, smallest, high):
    gain = 1.0
    for dim, blocks in cuts:
        steps = jax.random.uniform(jax.random.fold_in(jax.random.fold_in(key, 6), dim), (blocks,), jnp.float32, smallest / len(cuts), high / len(cuts))
        gain = gain * jnp.repeat(jnp.exp(steps), shape[dim] // blocks).reshape((-1,) + (1,) * (len(shape) - 1 - dim))
    return gain


def normal_values(key, shape, deviation, reach, split=(), kind=jnp.bfloat16):
    drawn = deviation * jax.random.normal(key, shape, jnp.float32)
    if split:
        drawn = drawn * block_scale(key, shape, split, -0.22, 0.18)
    return jnp.clip(drawn, -reach, reach).astype(kind)


def setup_inputs(seed: int = 0) -> dict:
    seeds = jax.random.split(jax.random.key(seed), 11)
    return {
        "start_state": normal_values(seeds[0], (F, NP), 1.0, 6.0, ((1, 16),), jnp.float32),
        "shocks": normal_values(seeds[1], (F, NP), 1.0, 6.0, ((1, 16),), jnp.float32),
        "drift_rate": jnp.clip(jax.random.uniform(seeds[2], (F,), jnp.float32, -0.5, 0.5), -0.5, 0.5),
        "vol_curve": jnp.clip(jnp.exp(jax.random.uniform(seeds[3], (F,), jnp.float32, math.log(0.2), math.log(1.0))), 0.2, 1.0),
        "weight_in": normal_values(seeds[4], (2, H, F), F ** -0.5, 0.625, ((0, 2),), jnp.float32),
        "bias_in": normal_values(seeds[5], (2, H), 0.5, 3.0, ((0, 2),), jnp.float32),
        "weight_out": normal_values(seeds[6], (2, H), H ** -0.5, 0.1875, ((0, 2),), jnp.float32),
        "default_date": touch_ends(jax.random.randint(seeds[7], (NP,), 1, 4), jax.random.fold_in(seeds[7], 1), 1, 3).astype(jnp.int32),
        "netting_set": touch_ends(jax.random.randint(seeds[8], (NP,), 0, S), jax.random.fold_in(seeds[8], 1), 0, S - 1).astype(jnp.int32),
        "loss_given": jnp.clip(jax.random.uniform(seeds[9], (S,), jnp.float32, 0.3, 0.9), 0.3, 0.9),
    }


step_dt = 0.25
root_dt = 0.5
growth_factor = 1.0075
fund_spread = 0.5
norm_eps = 1e-06

def net_parts(weight, bias, outer, start_state, shocks, drift_rate, vol_curve):
    hp = lax.Precision.HIGHEST
    next_state = start_state + drift_rate[:, None] * step_dt + vol_curve[:, None] * root_dt * shocks
    hidden_now = jnp.tanh(jnp.dot(weight, start_state, precision=hp) + bias[:, None])
    hidden_next = jnp.tanh(jnp.dot(weight, next_state, precision=hp) + bias[:, None])
    value_now = jnp.dot(outer, hidden_now, precision=hp)
    value_next = jnp.dot(outer, hidden_next, precision=hp)
    slope = outer[:, None] * (1.0 - hidden_now * hidden_now)
    delta = vol_curve[:, None] * jnp.dot(weight.T, slope, precision=hp)
    return (value_now, value_next, delta)

def block_loss(params, start_state, shocks, default_date, netting_set, loss_given, total):
    weight_in, bias_in, weight_out, drift_rate, vol_curve = params
    cn0, cn1, cz0 = net_parts(weight_in[0], bias_in[0], weight_out[0], start_state, shocks, drift_rate, vol_curve)
    xn0, xn1, xz0 = net_parts(weight_in[1], bias_in[1], weight_out[1], start_state, shocks, drift_rate, vol_curve)
    res_clean = cn1 - growth_factor * cn0 - root_dt * lax.optimization_barrier(jnp.sum(cz0 * shocks, axis=0))
    sets = jnp.arange(loss_given.shape[0], dtype=jnp.int32)
    loss_row = lax.optimization_barrier(jnp.sum(jnp.where(netting_set[None, :] == sets[:, None], loss_given[:, None], jnp.float32(0.0)), axis=0))
    margin = jnp.sqrt(lax.optimization_barrier(jnp.sum(cz0 * cz0, axis=0)) + norm_eps)
    target = jnp.where(default_date == 1, loss_row * jax.nn.softplus(cn1), xn1)
    res_xva = target - growth_factor * xn0 - root_dt * lax.optimization_barrier(jnp.sum(xz0 * shocks, axis=0)) + step_dt * fund_spread * margin
    loss = (jnp.sum(res_clean * res_clean) + jnp.sum(res_xva * res_xva)) / (2.0 * total)
    return (loss, jnp.stack([res_clean, res_xva]))

def reference(start_state, shocks, drift_rate, vol_curve, weight_in, bias_in, weight_out, default_date, netting_set, loss_given):
    total = start_state.shape[1]
    block = math.gcd(total, 4096)
    count = total // block
    feats = start_state.shape[0]
    state_blocks = start_state.reshape(feats, count, block).transpose(1, 0, 2)
    shock_blocks = shocks.reshape(feats, count, block).transpose(1, 0, 2)
    date_blocks = default_date.reshape(count, block)
    set_blocks = netting_set.reshape(count, block)
    params = (weight_in, bias_in, weight_out, drift_rate, vol_curve)
    grad_fn = jax.grad(block_loss, has_aux=True)

    def one_block(carry, items):
        state_b, shock_b, date_b, set_b = items
        grads, res = grad_fn(params, state_b, shock_b, date_b, set_b, loss_given, jnp.float32(total))
        return (jax.tree.map(lambda a, b: a + b, carry, grads), res)
    zeros = jax.tree.map(jnp.zeros_like, params)
    grads, res_blocks = lax.scan(one_block, zeros, (state_blocks, shock_blocks, date_blocks, set_blocks))
    residual = res_blocks.transpose(1, 0, 2).reshape(2, total)
    grad_w, grad_b, grad_o, grad_drift, grad_vol = grads
    count_w = grad_w.shape[1] * grad_w.shape[2] + 2 * grad_w.shape[1]
    sumsq = lax.optimization_barrier(jnp.sum(grad_w * grad_w, axis=(1, 2))) + lax.optimization_barrier(jnp.sum(grad_b * grad_b, axis=1)) + lax.optimization_barrier(jnp.sum(grad_o * grad_o, axis=1))
    scale = jnp.sqrt(sumsq / count_w + norm_eps)
    curve = jnp.stack([grad_drift, grad_vol])
    curve_step = curve / jnp.sqrt(jnp.mean(curve * curve) + norm_eps)
    return (residual, grad_w / scale[:, None, None], grad_b / scale[:, None], grad_o / scale[:, None], curve_step)
```

```python
import functools
import jax
import jax.numpy as jnp
from jax import lax
from jax.experimental import pallas as pl
from jax.experimental.pallas import tpu as pltpu
from jax.sharding import PartitionSpec as P

step_dt = 0.25
root_dt = 0.5
growth_factor = 1.0075
fund_spread = 0.5
norm_eps = 1e-06

f32 = jnp.float32
bf16 = jnp.bfloat16
LANES = 128
MESH = pl.DeviceIdType.MESH


def split(a):
    hi = a.astype(bf16)
    return hi, (a - hi.astype(f32)).astype(bf16)


def dot(a, b):
    return jnp.dot(a, b, preferred_element_type=f32)


def fold(a):
    return a[:, :LANES] + a[:, LANES:]


def wide(a, width):
    return jnp.concatenate([a] * (width // LANES), axis=1)


def kernel(
    n_path,
    reduce,
    start_ref,
    shock_ref,
    drift_ref,
    vol_ref,
    w_ref,
    bias_ref,
    outer_ref,
    date_ref,
    set_ref,
    given_ref,
    res_ref,
    *rest,
):
    if reduce:
        step_w_ref, step_b_ref, step_o_ref, curve_ref = rest[:4]
        rest = rest[4:]
    else:
        grad_ref, part_ref = rest[:2]
        rest = rest[2:]
    (
        x0,
        x1,
        sh,
        wp,
        wcat,
        wt,
        ocol,
        xcat,
        bt,
        h0s,
        h1s,
        s_hi,
        s_lo,
        dsum,
        x1sum,
        grad,
        swap_out,
        swap_in,
        swap_send,
        swap_recv,
        *rest,
    ) = rest
    feats, paths = start_ref.shape
    hidden = w_ref.shape[1]
    grp = lax.axis_index("grp")
    here = lax.axis_index("path")
    core = lax.rem(here, 2)
    chip = lax.div(here, 2)
    peers = n_path // 2
    half = hidden // 2
    other_grp = (1 - grp, here)
    other_core = (grp, chip * 2 + 1 - core)

    def peer(k):
        return lax.rem(chip + k, peers)

    barrier = pltpu.get_barrier_semaphore()
    pl.semaphore_signal(barrier, inc=1, device_id=other_grp, device_id_type=MESH)
    if reduce:
        pl.semaphore_signal(barrier, inc=1, device_id=other_core, device_id_type=MESH)
        for k in range(1, peers):
            pl.semaphore_signal(barrier, inc=1, device_id=(grp, peer(k) * 2 + core), device_id_type=MESH)

    rows = lax.broadcasted_iota(jnp.int32, (LANES, paths), 0)
    x0[...] = jnp.where(rows == feats, f32(1.0), f32(0.0))
    x0[0:feats, :] = start_ref[...]
    sh[...] = jnp.zeros_like(sh)
    sh[0:feats, :] = shock_ref[...]
    square = lax.broadcasted_iota(jnp.int32, (LANES, LANES), 0)
    curve_in = jnp.zeros((LANES, LANES), f32)
    pad = jnp.zeros((1, LANES - feats), f32)
    curve_in = jnp.where(square == 0, jnp.concatenate([drift_ref[...], pad], axis=1), curve_in)
    curve_in = jnp.where(square == 1, jnp.concatenate([vol_ref[...], pad], axis=1), curve_in)
    curve_col = curve_in.T
    drift = curve_col[:, 0:1]
    vol = curve_col[:, 1:2]
    shocks = sh[...]
    now = x0[...]
    nxt = now + drift * step_dt + vol * root_dt * shocks
    x1[...] = nxt
    for i, a in enumerate((now, nxt)):
        hi, lo = split(a)
        cols = slice(i * paths, (i + 1) * paths)
        xcat[0:LANES, cols] = hi
        xcat[LANES : 2 * LANES, cols] = hi
        xcat[2 * LANES :, cols] = lo
    wp[...] = jnp.zeros_like(wp)
    wp[:, 0:feats] = w_ref[0]
    dsum[...] = jnp.zeros_like(dsum)
    x1sum[...] = jnp.zeros_like(x1sum)

    def forward(j, carry):
        v0, v1 = carry
        base = pl.multiple_of(j * 2 * LANES, 2 * LANES)
        for k in range(2):
            r = pl.ds(pl.multiple_of(base + k * LANES, LANES), LANES)
            extra = jnp.where(square == feats, bias_ref[:, r], f32(0.0))
            extra = jnp.where(square == feats + 1, outer_ref[:, r], extra)
            w = wp[r, :]
            hi, lo = split(w.T)
            wt[0:LANES, r] = hi
            wt[LANES:, r] = lo
            extra = extra.T
            ocol[r, :] = jnp.broadcast_to(extra[:, feats + 1 : feats + 2], (LANES, LANES))
            hi, lo = split(w + extra)
            wcat[r, 0:LANES] = hi
            wcat[r, LANES : 2 * LANES] = lo
            wcat[r, 2 * LANES :] = hi
        r = pl.ds(base, 2 * LANES)
        z = dot(wcat[r, :], xcat[...])
        h0 = jnp.tanh(z[:, :paths])
        h1 = jnp.tanh(z[:, paths:])
        o = wide(ocol[r, :], paths)
        h0s[r, :] = h0
        h1s[r, :] = h1
        hi, lo = split(o * (1.0 - h0 * h0))
        s_hi[r, :] = hi
        s_lo[r, :] = lo
        d = dot(wt[:, r], hi)
        dsum[...] += d[:LANES] + d[LANES:] + dot(wt[0:LANES, r], lo)
        v0 = v0 + jnp.sum(o * h0, axis=0, keepdims=True)
        v1 = v1 + jnp.sum(o * h1, axis=0, keepdims=True)
        return v0, v1

    zero = jnp.zeros((1, paths), f32)
    v0, v1 = lax.fori_loop(0, hidden // (2 * LANES), forward, (zero, zero))
    inner = dsum[...]
    delta = vol * inner
    rest_own = -growth_factor * v0 - root_dt * jnp.sum(delta * shocks, axis=0, keepdims=True)
    square_own = jnp.sum(delta * delta, axis=0, keepdims=True)
    swap_out[0:1, :] = v1
    swap_out[1:2, :] = rest_own
    swap_out[2:3, :] = square_own
    swap_out[3:, :] = jnp.zeros((5, paths), f32)

    pl.semaphore_wait(barrier, peers + 1 if reduce else 1)
    swap = pltpu.make_async_remote_copy(
        src_ref=swap_out,
        dst_ref=swap_in,
        send_sem=swap_send.at[0],
        recv_sem=swap_recv.at[0],
        device_id=other_grp,
        device_id_type=MESH,
    )
    swap.start()
    for i, a in ((1, x0), (2, x1)):
        hi, lo = split(a[...].T)
        r = slice(i * paths, (i + 1) * paths)
        bt[r, 0:LANES] = hi
        bt[r, LANES:] = lo
    loss_row = zero
    for s in range(given_ref.shape[0]):
        loss_row = jnp.where(set_ref[...] == s, given_ref[s], loss_row)
    defaulted = date_ref[...] == 1
    clean = jnp.full((1, paths), grp, jnp.int32) == 0
    swap.wait()

    got_v1, got_rest, got_square = swap_in[0:1, :], swap_in[1:2, :], swap_in[2:3, :]
    clean_v1 = jnp.where(clean, v1, got_v1)
    res_clean = clean_v1 + jnp.where(clean, rest_own, got_rest)
    margin = jnp.sqrt(jnp.where(clean, square_own, got_square) + norm_eps)
    tail = jnp.exp(-jnp.abs(clean_v1))
    softplus = jnp.maximum(clean_v1, 0.0) + jnp.log1p(tail)
    sigmoid = jnp.where(clean_v1 >= 0.0, f32(1.0), tail) / (1.0 + tail)
    target = jnp.where(defaulted, loss_row * softplus, jnp.where(clean, got_v1, v1))
    res_xva = target + jnp.where(clean, got_rest, rest_own) + step_dt * fund_spread * margin
    residual = jnp.where(clean, res_clean, res_xva)
    res_ref[...] = residual
    per = f32(1.0 / (n_path * paths))
    weighted = residual * per
    weighted_xva = res_xva * per
    cot_now = -growth_factor * weighted
    cot_next = jnp.where(
        clean,
        weighted + jnp.where(defaulted, loss_row * sigmoid * weighted_xva, f32(0.0)),
        jnp.where(defaulted, f32(0.0), weighted),
    )
    pull = jnp.where(clean, step_dt * fund_spread * weighted_xva / margin, f32(0.0))
    cot_delta = -root_dt * weighted * shocks + pull * delta
    cot_inner = vol * cot_delta
    hi, lo = split(cot_inner)
    xcat[0:LANES, 0:paths] = hi
    xcat[LANES : 2 * LANES, 0:paths] = hi
    xcat[2 * LANES :, 0:paths] = lo
    hi, lo = split(cot_inner.T)
    bt[0:paths, 0:LANES] = hi
    bt[0:paths, LANES:] = lo
    lane = lax.broadcasted_iota(jnp.int32, (LANES, LANES), 1)

    def backward(base):
        r = pl.ds(pl.multiple_of(base, LANES), LANES)
        h0 = h0s[r, :]
        h1 = h1s[r, :]
        o = wide(ocol[r, :], paths)
        gap = 1.0 - h0 * h0
        t = dot(wcat[r, :], xcat[:, 0:paths])
        total = jnp.sum(t * gap + cot_now * h0 + cot_next * h1, axis=1, keepdims=True)
        y0_hi, y0_lo = split(o * gap * (cot_now - 2.0 * h0 * t))
        y1_hi, y1_lo = split(o * (1.0 - h1 * h1) * cot_next)
        a_hi = jnp.concatenate([s_hi[r, :], y0_hi, y1_hi], axis=1)
        a_lo = jnp.concatenate([s_lo[r, :], y0_lo, y1_lo], axis=1)
        g = fold(dot(a_hi, bt[...])) + dot(a_lo, bt[:, 0:LANES])
        grad[r, :] = g + jnp.where(lane == feats + 1, total, f32(0.0))
        back = dot(wt[:, r], y1_hi)
        x1sum[...] += back[:LANES] + back[LANES:] + dot(wt[0:LANES, r], y1_lo)

    def curve_rows():
        back = x1sum[...]
        by_drift = fold(step_dt * back).T
        by_vol = fold(root_dt * shocks * back + cot_delta * inner).T
        sub = lax.broadcasted_iota(jnp.int32, (8, LANES), 0)
        return jnp.where(
            sub == 0,
            jnp.sum(by_drift, axis=0, keepdims=True),
            jnp.where(sub == 1, jnp.sum(by_vol, axis=0, keepdims=True), f32(0.0)),
        )

    if not reduce:

        def whole_block(j, carry):
            backward(j * LANES)
            return carry

        lax.fori_loop(0, hidden // LANES, whole_block, 0)
        grad_ref[...] = grad[...]
        part_ref[...] = curve_rows()
        return

    (
        pair_in,
        peer_in,
        final,
        curve_out,
        curve_pair,
        curve_sum,
        curve_peer,
        curve_half,
        curve_far,
        pair_send,
        pair_recv,
        peer_send,
        peer_recv,
        all_send,
        all_recv,
        fwd_send,
        fwd_recv,
        curve_send,
        curve_recv,
        cpeer_send,
        cpeer_recv,
    ) = rest
    blocks = half // LANES
    chunk = half // peers
    per_block = LANES // chunk
    mine = core * half
    theirs = (1 - core) * half

    def turned(j):
        return lax.rem(j + 1 + lax.div(chip, per_block), blocks)

    def pair_copy(j):
        return pltpu.make_async_remote_copy(
            src_ref=grad.at[pl.ds(pl.multiple_of(theirs + j * LANES, LANES), LANES), :],
            dst_ref=pair_in.at[pl.ds(pl.multiple_of(j * LANES, LANES), LANES), :],
            send_sem=pair_send.at[j],
            recv_sem=pair_recv.at[j],
            device_id=other_core,
            device_id_type=MESH,
        )

    def chunk_rows(start, owner):
        return pl.ds(pl.multiple_of(start + owner * chunk, chunk), chunk)

    def peer_copy(owner, slot):
        return pltpu.make_async_remote_copy(
            src_ref=grad.at[chunk_rows(mine, owner), :],
            dst_ref=peer_in.at[slot],
            send_sem=peer_send.at[owner],
            recv_sem=peer_recv.at[slot],
            device_id=(grp, owner * 2 + core),
            device_id_type=MESH,
        )

    def all_copy(to, owner):
        return pltpu.make_async_remote_copy(
            src_ref=final.at[chunk_rows(mine, owner), :],
            dst_ref=final.at[chunk_rows(mine, owner), :],
            send_sem=all_send.at[to],
            recv_sem=all_recv.at[owner],
            device_id=(grp, to * 2 + core),
            device_id_type=MESH,
        )

    def fwd_copy(start, owner):
        return pltpu.make_async_remote_copy(
            src_ref=final.at[chunk_rows(start, owner), :],
            dst_ref=final.at[chunk_rows(start, owner), :],
            send_sem=fwd_send.at[owner],
            recv_sem=fwd_recv.at[owner],
            device_id=other_core,
            device_id_type=MESH,
        )

    def curve_copy(i, src, dst, to):
        return pltpu.make_async_remote_copy(
            src_ref=src,
            dst_ref=dst,
            send_sem=curve_send.at[i],
            recv_sem=curve_recv.at[i],
            device_id=to,
            device_id_type=MESH,
        )

    def cpeer_copy(to, slot):
        return pltpu.make_async_remote_copy(
            src_ref=curve_sum,
            dst_ref=curve_peer.at[slot],
            send_sem=cpeer_send.at[to],
            recv_sem=cpeer_recv.at[slot],
            device_id=(grp, to * 2 + core),
            device_id_type=MESH,
        )

    def their_block(j, carry):
        b = turned(j)
        backward(theirs + b * LANES)
        pair_copy(b).start()
        return carry

    def my_block(j, carry):
        b = turned(j)
        backward(mine + b * LANES)
        pair_copy(b).wait_recv()
        r = pl.ds(pl.multiple_of(mine + b * LANES, LANES), LANES)
        grad[r, :] += pair_in[pl.ds(pl.multiple_of(b * LANES, LANES), LANES), :]
        for k in range(per_block):
            owner = b * per_block + k

            @pl.when(owner != chip)
            def _():
                peer_copy(owner, chip).start()

        return carry

    lax.fori_loop(0, blocks, their_block, 0)
    lax.fori_loop(0, blocks, my_block, 0)
    curve_out[...] = curve_rows()
    pair_curve = curve_copy(0, curve_out, curve_pair, other_core)
    pair_curve.start()
    total = grad[chunk_rows(mine, chip), :]
    for k in range(1, peers):
        p = peer(k)
        peer_copy(p, p).wait_recv()
        total = total + peer_in[p]
    final[chunk_rows(mine, chip), :] = total
    for k in range(1, peers):
        all_copy(peer(k), chip).start()
    fwd_copy(mine, chip).start()
    pair_curve.wait_recv()
    curve_sum[...] = curve_out[...] + curve_pair[...]
    for k in range(1, peers):
        cpeer_copy(peer(k), chip).start()
    for k in range(1, peers):
        p = peer(k)
        all_copy(p, p).wait_recv()
        fwd_copy(mine, p).start()
    for p in range(peers):

        @pl.when(p != chip)
        def _():
            cpeer_copy(p, p).wait_recv()

        @pl.when(p == chip)
        def _():
            curve_peer[p] = curve_sum[...]

    curve = curve_peer[0]
    for p in range(1, peers):
        curve = curve + curve_peer[p]
    curve_half[...] = curve
    far_curve = curve_copy(1, curve_half, curve_far, other_grp)
    far_curve.start()
    for k in range(peers):
        fwd_copy(theirs, peer(k)).wait_recv()

    summed = final[...]
    parts = jnp.sum(jnp.sum(summed * summed, axis=0, keepdims=True), axis=1, keepdims=True)
    inverse = 1.0 / jnp.sqrt(parts / (hidden * feats + 2 * hidden) + norm_eps)
    step_w_ref[0] = final[:, 0:feats] * inverse
    for j in range(hidden // LANES):
        flipped = final[j * LANES : (j + 1) * LANES, :].T * inverse
        step_b_ref[:, j * LANES : (j + 1) * LANES] = flipped[feats : feats + 1, :]
        step_o_ref[:, j * LANES : (j + 1) * LANES] = flipped[feats + 1 : feats + 2, :]
    far_curve.wait_recv()
    curve = (curve_half[...] + curve_far[...])[0:2, 0:feats]
    mean = jnp.sum(jnp.sum(curve * curve, axis=0, keepdims=True), axis=1, keepdims=True) / (2 * feats)
    curve_ref[...] = curve / jnp.sqrt(mean + norm_eps)

    far_curve.wait_send()
    pair_curve.wait_send()
    for j in range(blocks):
        pair_copy(j).wait_send()
    for k in range(1, peers):
        peer_copy(peer(k), chip).wait_send()
        all_copy(peer(k), chip).wait_send()
        cpeer_copy(peer(k), chip).wait_send()
    for k in range(peers):
        fwd_copy(mine, peer(k)).wait_send()


def body(
    n_path,
    start_state,
    shocks,
    drift_rate,
    vol_curve,
    weight_in,
    bias_in,
    weight_out,
    default_date,
    netting_set,
    loss_given,
):
    feats, paths = start_state.shape
    hidden = weight_in.shape[1]
    peers = n_path // 2
    half = hidden // 2
    reduce = n_path % 2 == 0 and peers > 1 and half % (8 * peers) == 0 and half // peers <= LANES
    wide_row = (LANES, paths)
    tile = (8, LANES)
    scratch = [
        pltpu.VMEM(wide_row, f32),
        pltpu.VMEM(wide_row, f32),
        pltpu.VMEM(wide_row, f32),
        pltpu.VMEM((hidden, LANES), f32),
        pltpu.VMEM((hidden, 3 * LANES), bf16),
        pltpu.VMEM((2 * LANES, hidden), bf16),
        pltpu.VMEM((hidden, LANES), f32),
        pltpu.VMEM((3 * LANES, 2 * paths), bf16),
        pltpu.VMEM((3 * paths, 2 * LANES), bf16),
        pltpu.VMEM((hidden, paths), f32),
        pltpu.VMEM((hidden, paths), f32),
        pltpu.VMEM((hidden, paths), bf16),
        pltpu.VMEM((hidden, paths), bf16),
        pltpu.VMEM(wide_row, f32),
        pltpu.VMEM(wide_row, f32),
        pltpu.VMEM((hidden, LANES), f32),
        pltpu.VMEM((8, paths), f32),
        pltpu.VMEM((8, paths), f32),
        pltpu.SemaphoreType.DMA((1,)),
        pltpu.SemaphoreType.DMA((1,)),
    ]
    outs = [jax.ShapeDtypeStruct((1, paths), f32)]
    if reduce:
        blocks = half // LANES
        scratch += [
            pltpu.VMEM((half, LANES), f32),
            pltpu.VMEM((peers, half // peers, LANES), f32),
            pltpu.VMEM((hidden, LANES), f32),
            pltpu.VMEM(tile, f32),
            pltpu.VMEM(tile, f32),
            pltpu.VMEM(tile, f32),
            pltpu.VMEM((peers,) + tile, f32),
            pltpu.VMEM(tile, f32),
            pltpu.VMEM(tile, f32),
        ]
        scratch += [pltpu.SemaphoreType.DMA((blocks,))] * 2
        scratch += [pltpu.SemaphoreType.DMA((peers,))] * 6
        scratch += [pltpu.SemaphoreType.DMA((2,))] * 2
        scratch += [pltpu.SemaphoreType.DMA((peers,))] * 2
        outs += [
            jax.ShapeDtypeStruct((1, hidden, feats), f32),
            jax.ShapeDtypeStruct((1, hidden), f32),
            jax.ShapeDtypeStruct((1, hidden), f32),
            jax.ShapeDtypeStruct((2, feats), f32),
        ]
    else:
        outs += [jax.ShapeDtypeStruct((hidden, LANES), f32), jax.ShapeDtypeStruct(tile, f32)]
    vmem = pl.BlockSpec(memory_space=pltpu.VMEM)
    results = pl.pallas_call(
        functools.partial(kernel, n_path, reduce),
        out_shape=outs,
        in_specs=[vmem] * 9 + [pl.BlockSpec(memory_space=pltpu.SMEM)],
        out_specs=[vmem] * len(outs),
        scratch_shapes=scratch,
        compiler_params=pltpu.CompilerParams(
            collective_id=0, has_side_effects=True, vmem_limit_bytes=40 * 1024 * 1024
        ),
        name="bsde_step",
    )(
        start_state,
        shocks,
        drift_rate[None, :],
        vol_curve[None, :],
        weight_in,
        bias_in,
        weight_out,
        default_date[None, :],
        netting_set[None, :],
        loss_given,
    )
    if reduce:
        return tuple(results)
    residual, grad, part = results
    grad = lax.psum(grad, "path")
    curve = lax.psum(part, ("grp", "path"))[:2, :feats]
    scale = jnp.sqrt(jnp.sum(grad * grad) / (hidden * feats + 2 * hidden) + norm_eps)
    step = grad / scale
    curve_step = curve / jnp.sqrt(jnp.mean(curve * curve) + norm_eps)
    return (residual, step[None, :, :feats], step[None, :, feats], step[None, :, feats + 1], curve_step)


def solution(mesh):
    return jax.shard_map(
        functools.partial(body, mesh.shape["path"]),
        mesh=mesh,
        in_specs=(
            P(None, "path"),
            P(None, "path"),
            P(),
            P(),
            P("grp", None, None),
            P("grp", None),
            P("grp", None),
            P("path"),
            P("path"),
            P(),
        ),
        out_specs=(P("grp", "path"), P("grp", None, None), P("grp", None), P("grp", None), P()),
        check_vma=False,
    )
```

```python
import functools
import jax
import jax.numpy as jnp
from jax import lax
from jax.experimental import pallas as pl
from jax.experimental.pallas import tpu as pltpu
from jax.sharding import PartitionSpec as P

step_dt = 0.25
root_dt = 0.5
growth_factor = 1.0075
fund_spread = 0.5
norm_eps = 1e-06

f32 = jnp.float32
bf16 = jnp.bfloat16
LANES = 128
MESH = pl.DeviceIdType.MESH


def split(a):
    hi = a.astype(bf16)
    return hi, (a - hi.astype(f32)).astype(bf16)


def dot(a, b):
    return jnp.dot(a, b, preferred_element_type=f32)


def fold(a):
    return a[:, :LANES] + a[:, LANES:]


def wide(a, width):
    return jnp.concatenate([a] * (width // LANES), axis=1)


def kernel(
    n_path,
    reduce,
    start_ref,
    shock_ref,
    drift_ref,
    vol_ref,
    w_ref,
    bias_ref,
    outer_ref,
    date_ref,
    set_ref,
    given_ref,
    res_ref,
    *rest,
):
    sum_ref, curve_ref = rest[:2]
    rest = rest[2:]
    (
        x0,
        x1,
        sh,
        wp,
        wcat,
        wt,
        ocol,
        xcat,
        bt,
        h0s,
        h1s,
        s_hi,
        s_lo,
        dsum,
        x1sum,
        grad,
        swap_out,
        swap_in,
        swap_send,
        swap_recv,
        *rest,
    ) = rest
    feats, paths = start_ref.shape
    hidden = w_ref.shape[2]
    grp = lax.axis_index("grp")
    here = lax.axis_index("path")
    core = lax.rem(here, 2)
    chip = lax.div(here, 2)
    peers = n_path // 2
    half = hidden // 2
    other_grp = (1 - grp, here)
    other_core = (grp, chip * 2 + 1 - core)

    def peer(k):
        return lax.rem(chip + k, peers)

    barrier = pltpu.get_barrier_semaphore()
    pl.semaphore_signal(barrier, inc=1, device_id=other_grp, device_id_type=MESH)
    if reduce:
        pl.semaphore_signal(barrier, inc=1, device_id=other_core, device_id_type=MESH)
        for k in range(1, peers):
            pl.semaphore_signal(barrier, inc=1, device_id=(grp, peer(k) * 2 + core), device_id_type=MESH)

    rows = lax.broadcasted_iota(jnp.int32, (LANES, paths), 0)
    x0[...] = jnp.where(rows == feats, f32(1.0), f32(0.0))
    x0[0:feats, :] = start_ref[...]
    sh[...] = jnp.zeros_like(sh)
    sh[0:feats, :] = shock_ref[...]
    square = lax.broadcasted_iota(jnp.int32, (LANES, LANES), 0)
    curve_in = jnp.zeros((LANES, LANES), f32)
    pad = jnp.zeros((1, LANES - feats), f32)
    curve_in = jnp.where(square == 0, jnp.concatenate([drift_ref[...], pad], axis=1), curve_in)
    curve_in = jnp.where(square == 1, jnp.concatenate([vol_ref[...], pad], axis=1), curve_in)
    curve_col = curve_in.T
    drift = curve_col[:, 0:1]
    vol = curve_col[:, 1:2]
    shocks = sh[...]
    now = x0[...]
    nxt = now + drift * step_dt + vol * root_dt * shocks
    x1[...] = nxt
    for i, a in enumerate((now, nxt)):
        hi, lo = split(a)
        cols = slice(i * paths, (i + 1) * paths)
        xcat[0:LANES, cols] = hi
        xcat[LANES : 2 * LANES, cols] = hi
        xcat[2 * LANES :, cols] = lo
    tail_row = feats // 8 * 8
    wp[tail_row:, :] = jnp.zeros((LANES - tail_row, hidden), f32)
    wp[0:feats, :] = w_ref[:, 0, :]
    wp[feats : feats + 1, :] = bias_ref[...]
    wp[feats + 1 : feats + 2, :] = outer_ref[...]
    dsum[...] = jnp.zeros_like(dsum)
    x1sum[...] = jnp.zeros_like(x1sum)

    def forward(j, carry):
        v0, v1 = carry
        base = pl.multiple_of(j * 2 * LANES, 2 * LANES)
        for k in range(2):
            r = pl.ds(pl.multiple_of(base + k * LANES, LANES), LANES)
            w = wp[:, r]
            hi, lo = split(w)
            wt[0:LANES, r] = hi
            wt[LANES:, r] = lo
            w = w.T
            ocol[r, :] = jnp.broadcast_to(w[:, feats + 1 : feats + 2], (LANES, LANES))
            hi, lo = split(w)
            wcat[r, 0:LANES] = hi
            wcat[r, LANES : 2 * LANES] = lo
            wcat[r, 2 * LANES :] = hi
        r = pl.ds(base, 2 * LANES)
        z = dot(wcat[r, :], xcat[...])
        h0 = jnp.tanh(z[:, :paths])
        h1 = jnp.tanh(z[:, paths:])
        o = wide(ocol[r, :], paths)
        h0s[r, :] = h0
        h1s[r, :] = h1
        hi, lo = split(o * (1.0 - h0 * h0))
        s_hi[r, :] = hi
        s_lo[r, :] = lo
        d = dot(wt[:, r], hi)
        dsum[...] += d[:LANES] + d[LANES:] + dot(wt[0:LANES, r], lo)
        v0 = v0 + jnp.sum(o * h0, axis=0, keepdims=True)
        v1 = v1 + jnp.sum(o * h1, axis=0, keepdims=True)
        return v0, v1

    zero = jnp.zeros((1, paths), f32)
    v0, v1 = lax.fori_loop(0, hidden // (2 * LANES), forward, (zero, zero), unroll=2)
    inner = dsum[...]
    delta = vol * inner
    rest_own = -growth_factor * v0 - root_dt * jnp.sum(delta * shocks, axis=0, keepdims=True)
    square_own = jnp.sum(delta * delta, axis=0, keepdims=True)
    swap_out[0:1, :] = v1
    swap_out[1:2, :] = rest_own
    swap_out[2:3, :] = square_own
    swap_out[3:, :] = jnp.zeros((5, paths), f32)

    pl.semaphore_wait(barrier, peers + 1 if reduce else 1)
    swap = pltpu.make_async_remote_copy(
        src_ref=swap_out,
        dst_ref=swap_in,
        send_sem=swap_send.at[0],
        recv_sem=swap_recv.at[0],
        device_id=other_grp,
        device_id_type=MESH,
    )
    swap.start()
    for i, a in ((1, x0), (2, x1)):
        hi, lo = split(a[...].T)
        r = slice(i * paths, (i + 1) * paths)
        bt[r, 0:LANES] = hi
        bt[r, LANES:] = lo
    loss_row = zero
    for s in range(given_ref.shape[0]):
        loss_row = jnp.where(set_ref[...] == s, given_ref[s], loss_row)
    defaulted = date_ref[...] == 1
    clean = jnp.full((1, paths), grp, jnp.int32) == 0
    swap.wait()

    got_v1, got_rest, got_square = swap_in[0:1, :], swap_in[1:2, :], swap_in[2:3, :]
    clean_v1 = jnp.where(clean, v1, got_v1)
    res_clean = clean_v1 + jnp.where(clean, rest_own, got_rest)
    margin = jnp.sqrt(jnp.where(clean, square_own, got_square) + norm_eps)
    tail = jnp.exp(-jnp.abs(clean_v1))
    softplus = jnp.maximum(clean_v1, 0.0) + jnp.log1p(tail)
    sigmoid = jnp.where(clean_v1 >= 0.0, f32(1.0), tail) / (1.0 + tail)
    target = jnp.where(defaulted, loss_row * softplus, jnp.where(clean, got_v1, v1))
    res_xva = target + jnp.where(clean, got_rest, rest_own) + step_dt * fund_spread * margin
    residual = jnp.where(clean, res_clean, res_xva)
    res_ref[...] = residual
    per = f32(1.0 / (n_path * paths))
    weighted = residual * per
    weighted_xva = res_xva * per
    cot_now = -growth_factor * weighted
    cot_next = jnp.where(
        clean,
        weighted + jnp.where(defaulted, loss_row * sigmoid * weighted_xva, f32(0.0)),
        jnp.where(defaulted, f32(0.0), weighted),
    )
    pull = jnp.where(clean, step_dt * fund_spread * weighted_xva / margin, f32(0.0))
    cot_delta = -root_dt * weighted * shocks + pull * delta
    cot_inner = vol * cot_delta
    hi, lo = split(cot_inner)
    xcat[0:LANES, 0:paths] = hi
    xcat[LANES : 2 * LANES, 0:paths] = hi
    xcat[2 * LANES :, 0:paths] = lo
    hi, lo = split(cot_inner.T)
    bt[0:paths, 0:LANES] = hi
    bt[0:paths, LANES:] = lo
    lane = lax.broadcasted_iota(jnp.int32, (2 * LANES, LANES), 1)

    def backward(b):
        r = pl.ds(pl.multiple_of(b * LANES, 2 * LANES), 2 * LANES)
        h0 = h0s[r, :]
        h1 = h1s[r, :]
        o = wide(ocol[r, :], paths)
        gap = 1.0 - h0 * h0
        t = dot(wcat[r, :], xcat[:, 0:paths])
        total = jnp.sum(t * gap + cot_now * h0 + cot_next * h1, axis=1, keepdims=True)
        y0_hi, y0_lo = split(o * gap * (cot_now - 2.0 * h0 * t))
        y1_hi, y1_lo = split(o * (1.0 - h1 * h1) * cot_next)
        a_hi = jnp.concatenate([s_hi[r, :], y0_hi, y1_hi], axis=1)
        a_lo = jnp.concatenate([s_lo[r, :], y0_lo, y1_lo], axis=1)
        g = fold(dot(a_hi, bt[...])) + dot(a_lo, bt[:, 0:LANES])
        g = g + jnp.where(lane == feats + 1, total, f32(0.0))
        depth = grad.shape[1]
        grad[b] = g[:LANES].T[:depth]
        grad[b + 1] = g[LANES:].T[:depth]
        back = dot(wt[:, r], y1_hi)
        x1sum[...] += back[:LANES] + back[LANES:] + dot(wt[0:LANES, r], y1_lo)

    def curve_rows():
        back = x1sum[...]
        by_drift = fold(step_dt * back).T
        by_vol = fold(root_dt * shocks * back + cot_delta * inner).T
        sub = lax.broadcasted_iota(jnp.int32, (8, LANES), 0)
        return jnp.where(
            sub == 0,
            jnp.sum(by_drift, axis=0, keepdims=True),
            jnp.where(sub == 1, jnp.sum(by_vol, axis=0, keepdims=True), f32(0.0)),
        )

    if not reduce:

        def whole_block(j, carry):
            backward(j * 2)
            return carry

        lax.fori_loop(0, hidden // (2 * LANES), whole_block, 0)
        sum_ref[...] = grad[...]
        curve_ref[...] = curve_rows()
        return

    (
        pair_in,
        near_in,
        far_in,
        final,
        curve_out,
        curve_pair,
        curve_sum,
        curve_peer,
        curve_half,
        curve_far,
        pair_send,
        pair_recv,
        near_send,
        near_recv,
        far_send,
        far_recv,
        all_send,
        all_recv,
        fwd_send,
        fwd_recv,
        side_send,
        side_recv,
        curve_send,
        curve_recv,
        cpeer_send,
        cpeer_recv,
    ) = rest
    blocks = half // LANES
    own = blocks // 2
    chips = peers // 2
    per_block = chips // own
    chunk = grad.shape[1] // per_block
    side = lax.rem(chip, 2)
    place = lax.div(chip, 2)
    mine = core * blocks
    theirs = (1 - core) * blocks
    near = (grp, (place * 2 + 1 - side) * 2 + core)

    def far(k):
        return lax.rem(place + k, chips)

    def part(start, on, owner):
        return (
            start + on * own + lax.div(owner, per_block),
            pl.ds(pl.multiple_of(lax.rem(owner, per_block) * chunk, chunk), chunk),
        )

    def copy(src, dst, send, recv, to):
        return pltpu.make_async_remote_copy(
            src_ref=src, dst_ref=dst, send_sem=send, recv_sem=recv, device_id=to, device_id_type=MESH
        )

    def pair_copy(b):
        return copy(grad.at[theirs + b], pair_in.at[b], pair_send.at[b], pair_recv.at[b], other_core)

    def near_copy(i):
        block = mine + (1 - side) * own + i
        return copy(grad.at[block], near_in.at[i], near_send.at[i], near_recv.at[i], near)

    def far_copy(owner, slot):
        b, r = part(mine, side, owner)
        to = (grp, (owner * 2 + side) * 2 + core)
        return copy(grad.at[b, r], far_in.at[slot], far_send.at[owner], far_recv.at[slot], to)

    def all_copy(to, owner):
        b, r = part(mine, side, owner)
        to_device = (grp, (to * 2 + side) * 2 + core)
        return copy(final.at[b, r], final.at[b, r], all_send.at[to], all_recv.at[owner], to_device)

    def side_copy(on, owner):
        b, r = part(mine, on, owner)
        return copy(final.at[b, r], final.at[b, r], side_send.at[owner], side_recv.at[owner], near)

    def fwd_copy(start, on, owner):
        b, r = part(start, on, owner)
        i = on * chips + owner
        return copy(final.at[b, r], final.at[b, r], fwd_send.at[i], fwd_recv.at[i], other_core)

    def curve_copy(i, src, dst, to):
        return pltpu.make_async_remote_copy(
            src_ref=src,
            dst_ref=dst,
            send_sem=curve_send.at[i],
            recv_sem=curve_recv.at[i],
            device_id=to,
            device_id_type=MESH,
        )

    def cpeer_copy(to, slot):
        return pltpu.make_async_remote_copy(
            src_ref=curve_sum,
            dst_ref=curve_peer.at[slot],
            send_sem=cpeer_send.at[to],
            recv_sem=cpeer_recv.at[slot],
            device_id=(grp, to * 2 + core),
            device_id_type=MESH,
        )

    def their_blocks(j, carry):
        b = lax.rem((1 - side) * own + j * 2, blocks)
        backward(theirs + b)
        pair_copy(b).start()
        pair_copy(b + 1).start()
        return carry

    def near_blocks(j, carry):
        b = (1 - side) * own + j * 2
        backward(mine + b)
        for k in range(2):
            pair_copy(b + k).wait_recv()
            grad[mine + b + k] += pair_in[b + k]
            near_copy(j * 2 + k).start()
        return carry

    def my_blocks(j, carry):
        b = side * own + j * 2
        backward(mine + b)
        for k in range(2):
            pair_copy(b + k).wait_recv()
            near_copy(j * 2 + k).wait_recv()
            grad[mine + b + k] += pair_in[b + k] + near_in[j * 2 + k]
            for i in range(per_block):
                owner = (j * 2 + k) * per_block + i

                @pl.when(owner != place)
                def _():
                    far_copy(owner, place).start()

        return carry

    lax.fori_loop(0, blocks // 2, their_blocks, 0)
    lax.fori_loop(0, own // 2, near_blocks, 0)
    lax.fori_loop(0, own // 2, my_blocks, 0)
    curve_out[...] = curve_rows()
    pair_curve = curve_copy(0, curve_out, curve_pair, other_core)
    pair_curve.start()
    b, r = part(mine, side, place)
    total = grad[b, r]
    for k in range(1, chips):
        p = far(k)
        far_copy(p, p).wait_recv()
        total = total + far_in[p]
    final[b, r] = total
    for k in range(1, chips):
        all_copy(far(k), place).start()
    side_copy(side, place).start()
    fwd_copy(mine, side, place).start()
    pair_curve.wait_recv()
    curve_sum[...] = curve_out[...] + curve_pair[...]
    for k in range(1, peers):
        cpeer_copy(peer(k), chip).start()
    for k in range(1, chips):
        p = far(k)
        all_copy(p, p).wait_recv()
        side_copy(side, p).start()
        fwd_copy(mine, side, p).start()
    for k in range(chips):
        p = far(k)
        side_copy(1 - side, p).wait_recv()
        fwd_copy(mine, 1 - side, p).start()
    for p in range(peers):

        @pl.when(p != chip)
        def _():
            cpeer_copy(p, p).wait_recv()

        @pl.when(p == chip)
        def _():
            curve_peer[p] = curve_sum[...]

    curve = curve_peer[0]
    for p in range(1, peers):
        curve = curve + curve_peer[p]
    curve_half[...] = curve
    far_curve = curve_copy(1, curve_half, curve_far, other_grp)
    far_curve.start()
    for on in (side, 1 - side):
        for k in range(chips):
            fwd_copy(theirs, on, far(k)).wait_recv()
    sum_ref[...] = final[...]
    far_curve.wait_recv()
    curve_ref[...] = curve_half[...] + curve_far[...]

    far_curve.wait_send()
    pair_curve.wait_send()
    for j in range(blocks):
        pair_copy(j).wait_send()
    for j in range(own):
        near_copy(j).wait_send()
    for k in range(1, chips):
        far_copy(far(k), place).wait_send()
        all_copy(far(k), place).wait_send()
    for k in range(1, peers):
        cpeer_copy(peer(k), chip).wait_send()
    for k in range(chips):
        side_copy(side, far(k)).wait_send()
        fwd_copy(mine, side, far(k)).wait_send()
        fwd_copy(mine, 1 - side, far(k)).wait_send()


def finish(res_ref, sum_ref, part_ref, res_out, step_w_ref, step_b_ref, step_o_ref, curve_ref):
    feats, _, hidden = step_w_ref.shape
    res_out[...] = res_ref[...]
    squares = jnp.zeros(sum_ref.shape[1:], f32)
    for j in range(hidden // LANES):
        squares = squares + sum_ref[j] * sum_ref[j]
    squares = jnp.sum(jnp.sum(squares, axis=0, keepdims=True), axis=1, keepdims=True)
    inverse = 1.0 / jnp.sqrt(squares / (hidden * feats + 2 * hidden) + norm_eps)
    for j in range(hidden // LANES):
        r = slice(j * LANES, (j + 1) * LANES)
        step = sum_ref[j] * inverse
        step_w_ref[:, 0, r] = step[:feats]
        step_b_ref[:, r] = step[feats : feats + 1]
        step_o_ref[:, r] = step[feats + 1 : feats + 2]
    curve = part_ref[0:2, 0:feats]
    mean = jnp.sum(jnp.sum(curve * curve, axis=0, keepdims=True), axis=1, keepdims=True) / (2 * feats)
    curve_ref[...] = curve / jnp.sqrt(mean + norm_eps)


def body(
    n_path,
    start_state,
    shocks,
    drift_rate,
    vol_curve,
    weight_in,
    bias_in,
    weight_out,
    default_date,
    netting_set,
    loss_given,
):
    feats, paths = start_state.shape
    hidden = weight_in.shape[1]
    peers = n_path // 2
    half = hidden // 2
    blocks = half // LANES
    own = blocks // 2
    chips = peers // 2
    reduce = n_path % 4 == 0 and chips >= own and chips % own == 0 and chips // own <= 4
    split_rows = 8 * (chips // own if reduce else 1)
    depth = -(-(feats + 2) // split_rows) * split_rows
    sums = (hidden // LANES, depth, LANES)
    wide_row = (LANES, paths)
    tile = (8, LANES)
    scratch = [
        pltpu.VMEM(wide_row, f32),
        pltpu.VMEM(wide_row, f32),
        pltpu.VMEM(wide_row, f32),
        pltpu.VMEM((LANES, hidden), f32),
        pltpu.VMEM((hidden, 3 * LANES), bf16),
        pltpu.VMEM((2 * LANES, hidden), bf16),
        pltpu.VMEM((hidden, LANES), f32),
        pltpu.VMEM((3 * LANES, 2 * paths), bf16),
        pltpu.VMEM((3 * paths, 2 * LANES), bf16),
        pltpu.VMEM((hidden, paths), f32),
        pltpu.VMEM((hidden, paths), f32),
        pltpu.VMEM((hidden, paths), bf16),
        pltpu.VMEM((hidden, paths), bf16),
        pltpu.VMEM(wide_row, f32),
        pltpu.VMEM(wide_row, f32),
        pltpu.VMEM(sums, f32),
        pltpu.VMEM((8, paths), f32),
        pltpu.VMEM((8, paths), f32),
        pltpu.SemaphoreType.DMA((1,)),
        pltpu.SemaphoreType.DMA((1,)),
    ]
    outs = [
        jax.ShapeDtypeStruct((1, paths), f32),
        jax.ShapeDtypeStruct(sums, f32),
        jax.ShapeDtypeStruct(tile, f32),
    ]
    if reduce:
        scratch += [
            pltpu.VMEM((blocks,) + sums[1:], f32),
            pltpu.VMEM((own,) + sums[1:], f32),
            pltpu.VMEM((chips, depth * own // chips, LANES), f32),
            pltpu.VMEM(sums, f32),
            pltpu.VMEM(tile, f32),
            pltpu.VMEM(tile, f32),
            pltpu.VMEM(tile, f32),
            pltpu.VMEM((peers,) + tile, f32),
            pltpu.VMEM(tile, f32),
            pltpu.VMEM(tile, f32),
        ]
        scratch += [pltpu.SemaphoreType.DMA((blocks,))] * 2
        scratch += [pltpu.SemaphoreType.DMA((own,))] * 2
        scratch += [pltpu.SemaphoreType.DMA((chips,))] * 4
        scratch += [pltpu.SemaphoreType.DMA((peers,))] * 2
        scratch += [pltpu.SemaphoreType.DMA((chips,))] * 2
        scratch += [pltpu.SemaphoreType.DMA((2,))] * 2
        scratch += [pltpu.SemaphoreType.DMA((peers,))] * 2
    vmem = pl.BlockSpec(memory_space=pltpu.VMEM)
    residual, total, curve = pl.pallas_call(
        functools.partial(kernel, n_path, reduce),
        out_shape=outs,
        in_specs=[vmem] * 9 + [pl.BlockSpec(memory_space=pltpu.SMEM)],
        out_specs=[vmem] * len(outs),
        scratch_shapes=scratch,
        compiler_params=pltpu.CompilerParams(
            collective_id=0, has_side_effects=True, vmem_limit_bytes=40 * 1024 * 1024
        ),
        name="bsde_step",
    )(
        start_state,
        shocks,
        drift_rate[None, :],
        vol_curve[None, :],
        jnp.transpose(weight_in, (2, 0, 1)),
        bias_in,
        weight_out,
        default_date[None, :],
        netting_set[None, :],
        loss_given,
    )
    if not reduce:
        total = lax.psum(total, "path")
        curve = lax.psum(curve, ("grp", "path"))
    residual, step_w, step_b, step_o, curve_step = pl.pallas_call(
        finish,
        out_shape=[
            jax.ShapeDtypeStruct((1, paths), f32),
            jax.ShapeDtypeStruct((feats, 1, hidden), f32),
            jax.ShapeDtypeStruct((1, hidden), f32),
            jax.ShapeDtypeStruct((1, hidden), f32),
            jax.ShapeDtypeStruct((2, feats), f32),
        ],
        in_specs=[vmem] * 3,
        out_specs=[vmem] * 5,
        compiler_params=pltpu.CompilerParams(vmem_limit_bytes=16 * 1024 * 1024),
        name="normalize",
    )(residual, total, curve)
    return (residual, jnp.transpose(step_w, (1, 2, 0)), step_b, step_o, curve_step)


def solution(mesh):
    return jax.shard_map(
        functools.partial(body, mesh.shape["path"]),
        mesh=mesh,
        in_specs=(
            P(None, "path"),
            P(None, "path"),
            P(),
            P(),
            P("grp", None, None),
            P("grp", None),
            P("grp", None),
            P("path"),
            P("path"),
            P(),
        ),
        out_specs=(P("grp", "path"), P("grp", None, None), P("grp", None), P("grp", None), P()),
        check_vma=False,
    )
```

```python
import functools
import jax
import jax.numpy as jnp
from jax import lax
from jax.experimental import pallas as pl
from jax.experimental.pallas import tpu as pltpu
from jax.sharding import PartitionSpec as P

step_dt = 0.25
root_dt = 0.5
growth_factor = 1.0075
fund_spread = 0.5
norm_eps = 1e-06

f32 = jnp.float32
bf16 = jnp.bfloat16
LANES = 128
MESH = pl.DeviceIdType.MESH


def split(a):
    hi = a.astype(bf16)
    return hi, (a - hi.astype(f32)).astype(bf16)


def dot(a, b):
    return jnp.dot(a, b, preferred_element_type=f32)


def fold(a):
    return a[:, :LANES] + a[:, LANES:]


def wide(a, width):
    return jnp.concatenate([a] * (width // LANES), axis=1)


def kernel(
    n_path,
    reduce,
    *rest,
):
    inputs, rest = rest[:10], rest[10:]
    res_ref, sum_ref, curve_ref = rest[:3]
    local, load_sem, rest = rest[3:13], rest[13], rest[14:]
    start_ref, shock_ref, drift_ref, vol_ref, w_ref, bias_ref, outer_ref, date_ref, set_ref, given_ref = local
    (
        x0,
        x1,
        sh,
        wp,
        wcat,
        wt,
        ocol,
        xcat,
        bt,
        h0s,
        h1s,
        s_hi,
        s_lo,
        dsum,
        x1sum,
        grad,
        swap_out,
        swap_in,
        swap_send,
        swap_recv,
        *rest,
    ) = rest
    feats, paths = start_ref.shape
    hidden = w_ref.shape[1]
    grp = lax.axis_index("grp")
    here = lax.axis_index("path")
    core = lax.rem(here, 2)
    chip = lax.div(here, 2)
    peers = n_path // 2
    half = hidden // 2
    other_grp = (1 - grp, here)
    other_core = (grp, chip * 2 + 1 - core)

    def peer(k):
        return lax.rem(chip + k, peers)

    loads = [pltpu.make_async_copy(a.at[:, 0, :] if i == 4 else a, b, load_sem.at[i]) for i, (a, b) in enumerate(zip(inputs, local))]
    for load in loads:
        load.start()
    barrier = pltpu.get_barrier_semaphore()
    pl.semaphore_signal(barrier, inc=1, device_id=other_grp, device_id_type=MESH)
    if reduce:
        pl.semaphore_signal(barrier, inc=1, device_id=other_core, device_id_type=MESH)
        for k in range(1, peers):
            pl.semaphore_signal(barrier, inc=1, device_id=(grp, peer(k) * 2 + core), device_id_type=MESH)

    for load in loads:
        load.wait()

    rows = lax.broadcasted_iota(jnp.int32, (LANES, paths), 0)
    x0[...] = jnp.where(rows == feats, f32(1.0), f32(0.0))
    x0[0:feats, :] = start_ref[...]
    sh[...] = jnp.zeros_like(sh)
    sh[0:feats, :] = shock_ref[...]
    square = lax.broadcasted_iota(jnp.int32, (LANES, LANES), 0)
    curve_in = jnp.zeros((LANES, LANES), f32)
    pad = jnp.zeros((1, LANES - feats), f32)
    curve_in = jnp.where(square == 0, jnp.concatenate([drift_ref[...], pad], axis=1), curve_in)
    curve_in = jnp.where(square == 1, jnp.concatenate([vol_ref[...], pad], axis=1), curve_in)
    curve_col = curve_in.T
    drift = curve_col[:, 0:1]
    vol = curve_col[:, 1:2]
    shocks = sh[...]
    now = x0[...]
    nxt = now + drift * step_dt + vol * root_dt * shocks
    x1[...] = nxt
    for i, a in enumerate((now, nxt)):
        hi, lo = split(a)
        cols = slice(i * paths, (i + 1) * paths)
        xcat[0:LANES, cols] = hi
        xcat[LANES : 2 * LANES, cols] = hi
        xcat[2 * LANES :, cols] = lo
    tail_row = feats // 8 * 8
    wp[tail_row:, :] = jnp.zeros((LANES - tail_row, hidden), f32)
    wp[0:feats, :] = w_ref[...]
    wp[feats : feats + 1, :] = bias_ref[...]
    wp[feats + 1 : feats + 2, :] = outer_ref[...]
    dsum[...] = jnp.zeros_like(dsum)
    x1sum[...] = jnp.zeros_like(x1sum)

    def forward(j, carry):
        v0, v1 = carry
        base = pl.multiple_of(j * 2 * LANES, 2 * LANES)
        for k in range(2):
            r = pl.ds(pl.multiple_of(base + k * LANES, LANES), LANES)
            w = wp[:, r]
            hi, lo = split(w)
            wt[0:LANES, r] = hi
            wt[LANES:, r] = lo
            w = w.T
            ocol[r, :] = jnp.broadcast_to(w[:, feats + 1 : feats + 2], (LANES, LANES))
            hi, lo = split(w)
            wcat[r, 0:LANES] = hi
            wcat[r, LANES : 2 * LANES] = lo
            wcat[r, 2 * LANES :] = hi
        r = pl.ds(base, 2 * LANES)
        z = dot(wcat[r, :], xcat[...])
        h0 = jnp.tanh(z[:, :paths])
        h1 = jnp.tanh(z[:, paths:])
        o = wide(ocol[r, :], paths)
        h0s[r, :] = h0
        h1s[r, :] = h1
        hi, lo = split(o * (1.0 - h0 * h0))
        s_hi[r, :] = hi
        s_lo[r, :] = lo
        d = dot(wt[:, r], hi)
        dsum[...] += d[:LANES] + d[LANES:] + dot(wt[0:LANES, r], lo)
        v0 = v0 + jnp.sum(o * h0, axis=0, keepdims=True)
        v1 = v1 + jnp.sum(o * h1, axis=0, keepdims=True)
        return v0, v1

    zero = jnp.zeros((1, paths), f32)
    v0, v1 = lax.fori_loop(0, hidden // (2 * LANES), forward, (zero, zero), unroll=2)
    inner = dsum[...]
    delta = vol * inner
    rest_own = -growth_factor * v0 - root_dt * jnp.sum(delta * shocks, axis=0, keepdims=True)
    square_own = jnp.sum(delta * delta, axis=0, keepdims=True)
    swap_out[0:1, :] = v1
    swap_out[1:2, :] = rest_own
    swap_out[2:3, :] = square_own
    swap_out[3:, :] = jnp.zeros((5, paths), f32)

    pl.semaphore_wait(barrier, peers + 1 if reduce else 1)
    swap = pltpu.make_async_remote_copy(
        src_ref=swap_out,
        dst_ref=swap_in,
        send_sem=swap_send.at[0],
        recv_sem=swap_recv.at[0],
        device_id=other_grp,
        device_id_type=MESH,
    )
    swap.start()
    for i, a in ((1, x0), (2, x1)):
        hi, lo = split(a[...].T)
        r = slice(i * paths, (i + 1) * paths)
        bt[r, 0:LANES] = hi
        bt[r, LANES:] = lo
    loss_row = zero
    for s in range(given_ref.shape[1]):
        loss_row = jnp.where(set_ref[...] == s, given_ref[0:1, s : s + 1], loss_row)
    defaulted = date_ref[...] == 1
    clean = jnp.full((1, paths), grp, jnp.int32) == 0
    swap.wait()

    got_v1, got_rest, got_square = swap_in[0:1, :], swap_in[1:2, :], swap_in[2:3, :]
    clean_v1 = jnp.where(clean, v1, got_v1)
    res_clean = clean_v1 + jnp.where(clean, rest_own, got_rest)
    margin = jnp.sqrt(jnp.where(clean, square_own, got_square) + norm_eps)
    tail = jnp.exp(-jnp.abs(clean_v1))
    softplus = jnp.maximum(clean_v1, 0.0) + jnp.log1p(tail)
    sigmoid = jnp.where(clean_v1 >= 0.0, f32(1.0), tail) / (1.0 + tail)
    target = jnp.where(defaulted, loss_row * softplus, jnp.where(clean, got_v1, v1))
    res_xva = target + jnp.where(clean, got_rest, rest_own) + step_dt * fund_spread * margin
    residual = jnp.where(clean, res_clean, res_xva)
    res_ref[...] = residual
    per = f32(1.0 / (n_path * paths))
    weighted = residual * per
    weighted_xva = res_xva * per
    cot_now = -growth_factor * weighted
    cot_next = jnp.where(
        clean,
        weighted + jnp.where(defaulted, loss_row * sigmoid * weighted_xva, f32(0.0)),
        jnp.where(defaulted, f32(0.0), weighted),
    )
    pull = jnp.where(clean, step_dt * fund_spread * weighted_xva / margin, f32(0.0))
    cot_delta = -root_dt * weighted * shocks + pull * delta
    cot_inner = vol * cot_delta
    hi, lo = split(cot_inner)
    xcat[0:LANES, 0:paths] = hi
    xcat[LANES : 2 * LANES, 0:paths] = hi
    xcat[2 * LANES :, 0:paths] = lo
    hi, lo = split(cot_inner.T)
    bt[0:paths, 0:LANES] = hi
    bt[0:paths, LANES:] = lo
    lane = lax.broadcasted_iota(jnp.int32, (2 * LANES, LANES), 1)

    def backward(b):
        r = pl.ds(pl.multiple_of(b * LANES, 2 * LANES), 2 * LANES)
        h0 = h0s[r, :]
        h1 = h1s[r, :]
        o = wide(ocol[r, :], paths)
        gap = 1.0 - h0 * h0
        t = dot(wcat[r, :], xcat[:, 0:paths])
        total = jnp.sum(t * gap + cot_now * h0 + cot_next * h1, axis=1, keepdims=True)
        y0_hi, y0_lo = split(o * gap * (cot_now - 2.0 * h0 * t))
        y1_hi, y1_lo = split(o * (1.0 - h1 * h1) * cot_next)
        a_hi = jnp.concatenate([s_hi[r, :], y0_hi, y1_hi], axis=1)
        a_lo = jnp.concatenate([s_lo[r, :], y0_lo, y1_lo], axis=1)
        g = fold(dot(a_hi, bt[...])) + dot(a_lo, bt[:, 0:LANES])
        g = g + jnp.where(lane == feats + 1, total, f32(0.0))
        depth = grad.shape[1]
        grad[b] = g[:LANES].T[:depth]
        grad[b + 1] = g[LANES:].T[:depth]
        back = dot(wt[:, r], y1_hi)
        x1sum[...] += back[:LANES] + back[LANES:] + dot(wt[0:LANES, r], y1_lo)

    def curve_rows():
        back = x1sum[...]
        by_drift = fold(step_dt * back).T
        by_vol = fold(root_dt * shocks * back + cot_delta * inner).T
        sub = lax.broadcasted_iota(jnp.int32, (8, LANES), 0)
        return jnp.where(
            sub == 0,
            jnp.sum(by_drift, axis=0, keepdims=True),
            jnp.where(sub == 1, jnp.sum(by_vol, axis=0, keepdims=True), f32(0.0)),
        )

    if not reduce:

        def whole_block(j, carry):
            backward(j * 2)
            return carry

        lax.fori_loop(0, hidden // (2 * LANES), whole_block, 0)
        sum_ref[...] = grad[...]
        curve_ref[...] = curve_rows()
        return

    (
        pair_in,
        near_in,
        far_in,
        final,
        curve_out,
        curve_pair,
        curve_sum,
        curve_peer,
        curve_half,
        curve_far,
        pair_send,
        pair_recv,
        near_send,
        near_recv,
        far_send,
        far_recv,
        all_send,
        all_recv,
        fwd_send,
        fwd_recv,
        side_send,
        side_recv,
        curve_send,
        curve_recv,
        cpeer_send,
        cpeer_recv,
    ) = rest
    blocks = half // LANES
    own = blocks // 2
    chips = peers // 2
    per_block = chips // own
    chunk = grad.shape[1] // per_block
    side = lax.rem(chip, 2)
    place = lax.div(chip, 2)
    mine = core * blocks
    theirs = (1 - core) * blocks
    near = (grp, (place * 2 + 1 - side) * 2 + core)

    def far(k):
        return lax.rem(place + k, chips)

    def part(start, on, owner):
        return (
            start + on * own + lax.div(owner, per_block),
            pl.ds(pl.multiple_of(lax.rem(owner, per_block) * chunk, chunk), chunk),
        )

    def copy(src, dst, send, recv, to):
        return pltpu.make_async_remote_copy(
            src_ref=src, dst_ref=dst, send_sem=send, recv_sem=recv, device_id=to, device_id_type=MESH
        )

    def pair_copy(b):
        return copy(grad.at[theirs + b], pair_in.at[b], pair_send.at[b], pair_recv.at[b], other_core)

    def near_copy(i):
        block = mine + (1 - side) * own + i
        return copy(grad.at[block], near_in.at[i], near_send.at[i], near_recv.at[i], near)

    def far_copy(owner, slot):
        b, r = part(mine, side, owner)
        to = (grp, (owner * 2 + side) * 2 + core)
        return copy(grad.at[b, r], far_in.at[slot], far_send.at[owner], far_recv.at[slot], to)

    def all_copy(to, owner):
        b, r = part(mine, side, owner)
        to_device = (grp, (to * 2 + side) * 2 + core)
        return copy(final.at[b, r], final.at[b, r], all_send.at[to], all_recv.at[owner], to_device)

    def side_copy(on, owner):
        b, r = part(mine, on, owner)
        return copy(final.at[b, r], final.at[b, r], side_send.at[owner], side_recv.at[owner], near)

    def fwd_copy(start, on, owner):
        b, r = part(start, on, owner)
        i = on * chips + owner
        return copy(final.at[b, r], final.at[b, r], fwd_send.at[i], fwd_recv.at[i], other_core)

    def curve_copy(i, src, dst, to):
        return pltpu.make_async_remote_copy(
            src_ref=src,
            dst_ref=dst,
            send_sem=curve_send.at[i],
            recv_sem=curve_recv.at[i],
            device_id=to,
            device_id_type=MESH,
        )

    def cpeer_copy(to, slot):
        return pltpu.make_async_remote_copy(
            src_ref=curve_sum,
            dst_ref=curve_peer.at[slot],
            send_sem=cpeer_send.at[to],
            recv_sem=cpeer_recv.at[slot],
            device_id=(grp, to * 2 + core),
            device_id_type=MESH,
        )

    def their_blocks(j, carry):
        b = lax.rem((1 - side) * own + j * 2, blocks)
        backward(theirs + b)
        pair_copy(b).start()
        pair_copy(b + 1).start()
        return carry

    def near_blocks(j, carry):
        b = (1 - side) * own + j * 2
        backward(mine + b)
        for k in range(2):
            pair_copy(b + k).wait_recv()
            grad[mine + b + k] += pair_in[b + k]
            near_copy(j * 2 + k).start()
        return carry

    def my_blocks(j, carry):
        b = side * own + j * 2
        backward(mine + b)
        for k in range(2):
            pair_copy(b + k).wait_recv()
            near_copy(j * 2 + k).wait_recv()
            grad[mine + b + k] += pair_in[b + k] + near_in[j * 2 + k]
            for i in range(per_block):
                owner = (j * 2 + k) * per_block + i

                @pl.when(owner != place)
                def _():
                    far_copy(owner, place).start()

        return carry

    lax.fori_loop(0, blocks // 2, their_blocks, 0)
    lax.fori_loop(0, own // 2, near_blocks, 0)
    lax.fori_loop(0, own // 2, my_blocks, 0)
    curve_out[...] = curve_rows()
    pair_curve = curve_copy(0, curve_out, curve_pair, other_core)
    pair_curve.start()
    b, r = part(mine, side, place)
    total = grad[b, r]
    for k in range(1, chips):
        p = far(k)
        far_copy(p, p).wait_recv()
        total = total + far_in[p]
    final[b, r] = total
    for k in range(1, chips):
        all_copy(far(k), place).start()
    side_copy(side, place).start()
    fwd_copy(mine, side, place).start()
    pair_curve.wait_recv()
    curve_sum[...] = curve_out[...] + curve_pair[...]
    for k in range(1, peers):
        cpeer_copy(peer(k), chip).start()
    for k in range(1, chips):
        p = far(k)
        all_copy(p, p).wait_recv()
        side_copy(side, p).start()
        fwd_copy(mine, side, p).start()
    for k in range(chips):
        p = far(k)
        side_copy(1 - side, p).wait_recv()
        fwd_copy(mine, 1 - side, p).start()
    for p in range(peers):

        @pl.when(p != chip)
        def _():
            cpeer_copy(p, p).wait_recv()

        @pl.when(p == chip)
        def _():
            curve_peer[p] = curve_sum[...]

    curve = curve_peer[0]
    for p in range(1, peers):
        curve = curve + curve_peer[p]
    curve_half[...] = curve
    far_curve = curve_copy(1, curve_half, curve_far, other_grp)
    far_curve.start()
    for on in (side, 1 - side):
        for k in range(chips):
            fwd_copy(theirs, on, far(k)).wait_recv()
    sum_ref[...] = final[...]
    far_curve.wait_recv()
    curve_ref[...] = curve_half[...] + curve_far[...]

    far_curve.wait_send()
    pair_curve.wait_send()
    for j in range(blocks):
        pair_copy(j).wait_send()
    for j in range(own):
        near_copy(j).wait_send()
    for k in range(1, chips):
        far_copy(far(k), place).wait_send()
        all_copy(far(k), place).wait_send()
    for k in range(1, peers):
        cpeer_copy(peer(k), chip).wait_send()
    for k in range(chips):
        side_copy(side, far(k)).wait_send()
        fwd_copy(mine, side, far(k)).wait_send()
        fwd_copy(mine, 1 - side, far(k)).wait_send()


def finish(res_ref, sum_ref, part_ref, res_out, step_w_ref, step_b_ref, step_o_ref, curve_ref):
    feats, _, hidden = step_w_ref.shape
    res_out[...] = res_ref[...]
    squares = jnp.zeros(sum_ref.shape[1:], f32)
    for j in range(hidden // LANES):
        squares = squares + sum_ref[j] * sum_ref[j]
    squares = jnp.sum(jnp.sum(squares, axis=0, keepdims=True), axis=1, keepdims=True)
    inverse = 1.0 / jnp.sqrt(squares / (hidden * feats + 2 * hidden) + norm_eps)
    for j in range(hidden // LANES):
        r = slice(j * LANES, (j + 1) * LANES)
        step = sum_ref[j] * inverse
        step_w_ref[:, 0, r] = step[:feats]
        step_b_ref[:, r] = step[feats : feats + 1]
        step_o_ref[:, r] = step[feats + 1 : feats + 2]
    curve = part_ref[0:2, 0:feats]
    mean = jnp.sum(jnp.sum(curve * curve, axis=0, keepdims=True), axis=1, keepdims=True) / (2 * feats)
    curve_ref[...] = curve / jnp.sqrt(mean + norm_eps)


def body(
    n_path,
    start_state,
    shocks,
    drift_rate,
    vol_curve,
    weight_in,
    bias_in,
    weight_out,
    default_date,
    netting_set,
    loss_given,
):
    feats, paths = start_state.shape
    hidden = weight_in.shape[1]
    peers = n_path // 2
    half = hidden // 2
    blocks = half // LANES
    own = blocks // 2
    chips = peers // 2
    reduce = n_path % 4 == 0 and chips >= own and chips % own == 0 and chips // own <= 4
    split_rows = 8 * (chips // own if reduce else 1)
    depth = -(-(feats + 2) // split_rows) * split_rows
    sums = (hidden // LANES, depth, LANES)
    wide_row = (LANES, paths)
    tile = (8, LANES)
    inputs = [
        start_state,
        shocks,
        drift_rate[None, :],
        vol_curve[None, :],
        jnp.transpose(weight_in, (2, 0, 1)),
        bias_in,
        weight_out,
        default_date[None, :],
        netting_set[None, :],
        loss_given[None, :],
    ]
    scratch = [pltpu.VMEM((feats, hidden) if a.ndim == 3 else a.shape, a.dtype) for a in inputs]
    scratch += [
        pltpu.SemaphoreType.DMA((len(inputs),)),
        pltpu.VMEM(wide_row, f32),
        pltpu.VMEM(wide_row, f32),
        pltpu.VMEM(wide_row, f32),
        pltpu.VMEM((LANES, hidden), f32),
        pltpu.VMEM((hidden, 3 * LANES), bf16),
        pltpu.VMEM((2 * LANES, hidden), bf16),
        pltpu.VMEM((hidden, LANES), f32),
        pltpu.VMEM((3 * LANES, 2 * paths), bf16),
        pltpu.VMEM((3 * paths, 2 * LANES), bf16),
        pltpu.VMEM((hidden, paths), f32),
        pltpu.VMEM((hidden, paths), f32),
        pltpu.VMEM((hidden, paths), bf16),
        pltpu.VMEM((hidden, paths), bf16),
        pltpu.VMEM(wide_row, f32),
        pltpu.VMEM(wide_row, f32),
        pltpu.VMEM(sums, f32),
        pltpu.VMEM((8, paths), f32),
        pltpu.VMEM((8, paths), f32),
        pltpu.SemaphoreType.DMA((1,)),
        pltpu.SemaphoreType.DMA((1,)),
    ]
    outs = [
        jax.ShapeDtypeStruct((1, paths), f32),
        jax.ShapeDtypeStruct(sums, f32),
        jax.ShapeDtypeStruct(tile, f32),
    ]
    if reduce:
        scratch += [
            pltpu.VMEM((blocks,) + sums[1:], f32),
            pltpu.VMEM((own,) + sums[1:], f32),
            pltpu.VMEM((chips, depth * own // chips, LANES), f32),
            pltpu.VMEM(sums, f32),
            pltpu.VMEM(tile, f32),
            pltpu.VMEM(tile, f32),
            pltpu.VMEM(tile, f32),
            pltpu.VMEM((peers,) + tile, f32),
            pltpu.VMEM(tile, f32),
            pltpu.VMEM(tile, f32),
        ]
        scratch += [pltpu.SemaphoreType.DMA((blocks,))] * 2
        scratch += [pltpu.SemaphoreType.DMA((own,))] * 2
        scratch += [pltpu.SemaphoreType.DMA((chips,))] * 4
        scratch += [pltpu.SemaphoreType.DMA((peers,))] * 2
        scratch += [pltpu.SemaphoreType.DMA((chips,))] * 2
        scratch += [pltpu.SemaphoreType.DMA((2,))] * 2
        scratch += [pltpu.SemaphoreType.DMA((peers,))] * 2
    vmem = pl.BlockSpec(memory_space=pltpu.VMEM)
    residual, total, curve = pl.pallas_call(
        functools.partial(kernel, n_path, reduce),
        out_shape=outs,
        in_specs=[pl.BlockSpec(memory_space=pltpu.HBM)] * len(inputs),
        out_specs=[vmem] * len(outs),
        scratch_shapes=scratch,
        compiler_params=pltpu.CompilerParams(
            collective_id=0, has_side_effects=True, vmem_limit_bytes=40 * 1024 * 1024
        ),
        name="bsde_step",
    )(*inputs)
    if not reduce:
        total = lax.psum(total, "path")
        curve = lax.psum(curve, ("grp", "path"))
    residual, step_w, step_b, step_o, curve_step = pl.pallas_call(
        finish,
        out_shape=[
            jax.ShapeDtypeStruct((1, paths), f32),
            jax.ShapeDtypeStruct((feats, 1, hidden), f32),
            jax.ShapeDtypeStruct((1, hidden), f32),
            jax.ShapeDtypeStruct((1, hidden), f32),
            jax.ShapeDtypeStruct((2, feats), f32),
        ],
        in_specs=[vmem] * 3,
        out_specs=[vmem] * 5,
        compiler_params=pltpu.CompilerParams(vmem_limit_bytes=16 * 1024 * 1024),
        name="normalize",
    )(residual, total, curve)
    return (residual, jnp.transpose(step_w, (1, 2, 0)), step_b, step_o, curve_step)


def solution(mesh):
    return jax.shard_map(
        functools.partial(body, mesh.shape["path"]),
        mesh=mesh,
        in_specs=(
            P(None, "path"),
            P(None, "path"),
            P(),
            P(),
            P("grp", None, None),
            P("grp", None),
            P("grp", None),
            P("path"),
            P("path"),
            P(),
        ),
        out_specs=(P("grp", "path"), P("grp", None, None), P("grp", None), P("grp", None), P()),
        check_vma=False,
    )
```

```python
import functools
import jax
import jax.numpy as jnp
from jax import lax
from jax.experimental import pallas as pl
from jax.experimental.pallas import tpu as pltpu
from jax.sharding import PartitionSpec as P

step_dt = 0.25
root_dt = 0.5
growth_factor = 1.0075
fund_spread = 0.5
norm_eps = 1e-06

f32 = jnp.float32
bf16 = jnp.bfloat16
LANES = 128
MESH = pl.DeviceIdType.MESH


def split(a):
    hi = a.astype(bf16)
    return hi, (a - hi.astype(f32)).astype(bf16)


def dot(a, b):
    return jnp.dot(a, b, preferred_element_type=f32)


def fold(a):
    return a[:, :LANES] + a[:, LANES:]


def wide(a, width):
    return jnp.concatenate([a] * (width // LANES), axis=1)


def kernel(
    n_path,
    reduce,
    *rest,
):
    inputs, rest = rest[:10], rest[10:]
    res_ref, sum_ref, curve_ref = rest[:3]
    local, load_sem, rest = rest[3:13], rest[13], rest[14:]
    start_ref, shock_ref, drift_ref, vol_ref, w_ref, bias_ref, outer_ref, date_ref, set_ref, given_ref = local
    (
        x0,
        x1,
        sh,
        wp,
        wcat,
        wt,
        ocol,
        xcat,
        bt,
        h0s,
        h1s,
        s_hi,
        s_lo,
        dsum,
        x1sum,
        grad,
        swap_out,
        swap_in,
        swap_send,
        swap_recv,
        *rest,
    ) = rest
    feats, paths = start_ref.shape
    hidden = w_ref.shape[1]
    grp = lax.axis_index("grp")
    here = lax.axis_index("path")
    core = lax.rem(here, 2)
    chip = lax.div(here, 2)
    peers = n_path // 2
    half = hidden // 2
    other_grp = (1 - grp, here)
    other_core = (grp, chip * 2 + 1 - core)

    def peer(k):
        return lax.rem(chip + k, peers)

    loads = [pltpu.make_async_copy(a.at[:, 0, :] if i == 4 else a, b, load_sem.at[i]) for i, (a, b) in enumerate(zip(inputs, local))]
    for load in loads:
        load.start()
    barrier = pltpu.get_barrier_semaphore()
    pl.semaphore_signal(barrier, inc=1, device_id=other_grp, device_id_type=MESH)
    if reduce:
        pl.semaphore_signal(barrier, inc=1, device_id=other_core, device_id_type=MESH)
        for k in range(1, peers):
            pl.semaphore_signal(barrier, inc=1, device_id=(grp, peer(k) * 2 + core), device_id_type=MESH)

    for load in loads:
        load.wait()

    rows = lax.broadcasted_iota(jnp.int32, (LANES, paths), 0)
    x0[...] = jnp.where(rows == feats, f32(1.0), f32(0.0))
    x0[0:feats, :] = start_ref[...]
    sh[...] = jnp.zeros_like(sh)
    sh[0:feats, :] = shock_ref[...]
    square = lax.broadcasted_iota(jnp.int32, (LANES, LANES), 0)
    curve_in = jnp.zeros((LANES, LANES), f32)
    pad = jnp.zeros((1, LANES - feats), f32)
    curve_in = jnp.where(square == 0, jnp.concatenate([drift_ref[...], pad], axis=1), curve_in)
    curve_in = jnp.where(square == 1, jnp.concatenate([vol_ref[...], pad], axis=1), curve_in)
    curve_col = curve_in.T
    drift = curve_col[:, 0:1]
    vol = curve_col[:, 1:2]
    shocks = sh[...]
    now = x0[...]
    nxt = now + drift * step_dt + vol * root_dt * shocks
    x1[...] = nxt
    for i, a in enumerate((now, nxt)):
        hi, lo = split(a)
        cols = slice(i * paths, (i + 1) * paths)
        xcat[0:LANES, cols] = hi
        xcat[LANES : 2 * LANES, cols] = hi
        xcat[2 * LANES :, cols] = lo
    tail_row = feats // 8 * 8
    wp[tail_row:, :] = jnp.zeros((LANES - tail_row, hidden), f32)
    wp[0:feats, :] = w_ref[...]
    wp[feats : feats + 1, :] = bias_ref[...]
    wp[feats + 1 : feats + 2, :] = outer_ref[...]
    dsum[...] = jnp.zeros_like(dsum)
    x1sum[...] = jnp.zeros_like(x1sum)

    def forward(j, carry):
        v0, v1 = carry
        base = pl.multiple_of(j * 2 * LANES, 2 * LANES)
        for k in range(2):
            r = pl.ds(pl.multiple_of(base + k * LANES, LANES), LANES)
            w = wp[:, r]
            hi, lo = split(w)
            wt[0:LANES, r] = hi
            wt[LANES:, r] = lo
            w = w.T
            ocol[r, :] = jnp.broadcast_to(w[:, feats + 1 : feats + 2], (LANES, LANES))
            hi, lo = split(w)
            wcat[r, 0:LANES] = hi
            wcat[r, LANES : 2 * LANES] = lo
            wcat[r, 2 * LANES :] = hi
        r = pl.ds(base, 2 * LANES)
        z = dot(wcat[r, :], xcat[...])
        h0 = jnp.tanh(z[:, :paths])
        h1 = jnp.tanh(z[:, paths:])
        o = wide(ocol[r, :], paths)
        h0s[r, :] = h0
        h1s[r, :] = h1
        hi, lo = split(o * (1.0 - h0 * h0))
        s_hi[r, :] = hi
        s_lo[r, :] = lo
        d = dot(wt[:, r], hi)
        dsum[...] += d[:LANES] + d[LANES:] + dot(wt[0:LANES, r], lo)
        v0 = v0 + jnp.sum(o * h0, axis=0, keepdims=True)
        v1 = v1 + jnp.sum(o * h1, axis=0, keepdims=True)
        return v0, v1

    zero = jnp.zeros((1, paths), f32)
    v0, v1 = lax.fori_loop(0, hidden // (2 * LANES), forward, (zero, zero), unroll=2)
    inner = dsum[...]
    delta = vol * inner
    rest_own = -growth_factor * v0 - root_dt * jnp.sum(delta * shocks, axis=0, keepdims=True)
    square_own = jnp.sum(delta * delta, axis=0, keepdims=True)
    swap_out[0:1, :] = v1
    swap_out[1:2, :] = rest_own
    swap_out[2:3, :] = square_own
    swap_out[3:, :] = jnp.zeros((5, paths), f32)

    pl.semaphore_wait(barrier, peers + 1 if reduce else 1)
    swap = pltpu.make_async_remote_copy(
        src_ref=swap_out,
        dst_ref=swap_in,
        send_sem=swap_send.at[0],
        recv_sem=swap_recv.at[0],
        device_id=other_grp,
        device_id_type=MESH,
    )
    swap.start()
    for i, a in ((1, x0), (2, x1)):
        hi, lo = split(a[...].T)
        r = slice(i * paths, (i + 1) * paths)
        bt[r, 0:LANES] = hi
        bt[r, LANES:] = lo
    loss_row = zero
    for s in range(given_ref.shape[1]):
        loss_row = jnp.where(set_ref[...] == s, given_ref[0:1, s : s + 1], loss_row)
    defaulted = date_ref[...] == 1
    clean = jnp.full((1, paths), grp, jnp.int32) == 0
    swap.wait()

    got_v1, got_rest, got_square = swap_in[0:1, :], swap_in[1:2, :], swap_in[2:3, :]
    clean_v1 = jnp.where(clean, v1, got_v1)
    res_clean = clean_v1 + jnp.where(clean, rest_own, got_rest)
    margin = jnp.sqrt(jnp.where(clean, square_own, got_square) + norm_eps)
    tail = jnp.exp(-jnp.abs(clean_v1))
    softplus = jnp.maximum(clean_v1, 0.0) + jnp.log1p(tail)
    sigmoid = jnp.where(clean_v1 >= 0.0, f32(1.0), tail) / (1.0 + tail)
    target = jnp.where(defaulted, loss_row * softplus, jnp.where(clean, got_v1, v1))
    res_xva = target + jnp.where(clean, got_rest, rest_own) + step_dt * fund_spread * margin
    residual = jnp.where(clean, res_clean, res_xva)
    res_ref[...] = residual
    per = f32(1.0 / (n_path * paths))
    weighted = residual * per
    weighted_xva = res_xva * per
    cot_now = -growth_factor * weighted
    cot_next = jnp.where(
        clean,
        weighted + jnp.where(defaulted, loss_row * sigmoid * weighted_xva, f32(0.0)),
        jnp.where(defaulted, f32(0.0), weighted),
    )
    pull = jnp.where(clean, step_dt * fund_spread * weighted_xva / margin, f32(0.0))
    cot_delta = -root_dt * weighted * shocks + pull * delta
    cot_inner = vol * cot_delta
    hi, lo = split(cot_inner)
    xcat[0:LANES, 0:paths] = hi
    xcat[LANES : 2 * LANES, 0:paths] = hi
    xcat[2 * LANES :, 0:paths] = lo
    hi, lo = split(cot_inner.T)
    bt[0:paths, 0:LANES] = hi
    bt[0:paths, LANES:] = lo
    lane = lax.broadcasted_iota(jnp.int32, (2 * LANES, LANES), 1)

    def backward(b):
        r = pl.ds(pl.multiple_of(b * LANES, 2 * LANES), 2 * LANES)
        h0 = h0s[r, :]
        h1 = h1s[r, :]
        o = wide(ocol[r, :], paths)
        gap = 1.0 - h0 * h0
        t = dot(wcat[r, :], xcat[:, 0:paths])
        total = jnp.sum(t * gap + cot_now * h0 + cot_next * h1, axis=1, keepdims=True)
        y0_hi, y0_lo = split(o * gap * (cot_now - 2.0 * h0 * t))
        y1_hi, y1_lo = split(o * (1.0 - h1 * h1) * cot_next)
        a_hi = jnp.concatenate([s_hi[r, :], y0_hi, y1_hi], axis=1)
        a_lo = jnp.concatenate([s_lo[r, :], y0_lo, y1_lo], axis=1)
        g = fold(dot(a_hi, bt[...])) + dot(a_lo, bt[:, 0:LANES])
        g = g + jnp.where(lane == feats + 1, total, f32(0.0))
        depth = grad.shape[1]
        grad[b] = g[:LANES].T[:depth]
        grad[b + 1] = g[LANES:].T[:depth]
        back = dot(wt[:, r], y1_hi)
        x1sum[...] += back[:LANES] + back[LANES:] + dot(wt[0:LANES, r], y1_lo)

    def curve_rows():
        back = x1sum[...]
        by_drift = fold(step_dt * back).T
        by_vol = fold(root_dt * shocks * back + cot_delta * inner).T
        sub = lax.broadcasted_iota(jnp.int32, (8, LANES), 0)
        return jnp.where(
            sub == 0,
            jnp.sum(by_drift, axis=0, keepdims=True),
            jnp.where(sub == 1, jnp.sum(by_vol, axis=0, keepdims=True), f32(0.0)),
        )

    if not reduce:

        def whole_block(j, carry):
            backward(j * 2)
            return carry

        lax.fori_loop(0, hidden // (2 * LANES), whole_block, 0)
        sum_ref[...] = grad[...]
        curve_ref[...] = curve_rows()
        return

    (
        pair_in,
        near_in,
        far_in,
        final,
        curve_out,
        curve_pair,
        curve_sum,
        curve_peer,
        curve_half,
        curve_far,
        pair_send,
        pair_recv,
        near_send,
        near_recv,
        far_send,
        far_recv,
        all_send,
        all_recv,
        fwd_send,
        fwd_recv,
        side_send,
        side_recv,
        curve_send,
        curve_recv,
        cpeer_send,
        cpeer_recv,
    ) = rest
    blocks = half // LANES
    own = blocks // 2
    chips = peers // 2
    per_block = chips // own
    chunk = grad.shape[1] // per_block
    side = lax.rem(chip, 2)
    place = lax.div(chip, 2)
    mine = core * blocks
    theirs = (1 - core) * blocks
    near = (grp, (place * 2 + 1 - side) * 2 + core)

    def far(k):
        return lax.rem(place + k, chips)

    def part(start, on, owner):
        return (
            start + on * own + lax.div(owner, per_block),
            pl.ds(pl.multiple_of(lax.rem(owner, per_block) * chunk, chunk), chunk),
        )

    def copy(src, dst, send, recv, to):
        return pltpu.make_async_remote_copy(
            src_ref=src, dst_ref=dst, send_sem=send, recv_sem=recv, device_id=to, device_id_type=MESH
        )

    def pair_copy(b):
        return copy(grad.at[theirs + b], pair_in.at[b], pair_send.at[b], pair_recv.at[b], other_core)

    def near_copy(i):
        block = mine + (1 - side) * own + i
        return copy(grad.at[block], near_in.at[i], near_send.at[i], near_recv.at[i], near)

    def far_copy(owner, slot):
        b, r = part(mine, side, owner)
        to = (grp, (owner * 2 + side) * 2 + core)
        return copy(grad.at[b, r], far_in.at[slot], far_send.at[owner], far_recv.at[slot], to)

    def all_copy(to, owner):
        b, r = part(mine, side, owner)
        to_device = (grp, (to * 2 + side) * 2 + core)
        return copy(final.at[b, r], final.at[b, r], all_send.at[to], all_recv.at[owner], to_device)

    def side_copy(on, owner):
        b, r = part(mine, on, owner)
        return copy(final.at[b, r], final.at[b, r], side_send.at[owner], side_recv.at[owner], near)

    def fwd_copy(start, on, owner):
        b, r = part(start, on, owner)
        i = on * chips + owner
        return copy(final.at[b, r], final.at[b, r], fwd_send.at[i], fwd_recv.at[i], other_core)

    def curve_copy(i, src, dst, to):
        return pltpu.make_async_remote_copy(
            src_ref=src,
            dst_ref=dst,
            send_sem=curve_send.at[i],
            recv_sem=curve_recv.at[i],
            device_id=to,
            device_id_type=MESH,
        )

    def cpeer_copy(to, slot):
        return pltpu.make_async_remote_copy(
            src_ref=curve_sum,
            dst_ref=curve_peer.at[slot],
            send_sem=cpeer_send.at[to],
            recv_sem=cpeer_recv.at[slot],
            device_id=(grp, to * 2 + core),
            device_id_type=MESH,
        )

    def their_blocks(j, carry):
        b = lax.rem((1 - side) * own + j * 2, blocks)
        backward(theirs + b)
        pair_copy(b).start()
        pair_copy(b + 1).start()
        return carry

    def near_blocks(j, carry):
        b = (1 - side) * own + j * 2
        backward(mine + b)
        for k in range(2):
            pair_copy(b + k).wait_recv()
            grad[mine + b + k] += pair_in[b + k]
            near_copy(j * 2 + k).start()
        return carry

    def my_blocks(j, carry):
        b = side * own + j * 2
        backward(mine + b)
        for k in range(2):
            pair_copy(b + k).wait_recv()
            near_copy(j * 2 + k).wait_recv()
            grad[mine + b + k] += pair_in[b + k] + near_in[j * 2 + k]
            for i in range(per_block):
                owner = (j * 2 + k) * per_block + i

                @pl.when(owner != place)
                def _():
                    far_copy(owner, place).start()

        return carry

    lax.fori_loop(0, blocks // 2, their_blocks, 0)
    lax.fori_loop(0, own // 2, near_blocks, 0)
    lax.fori_loop(0, own // 2, my_blocks, 0)
    curve_out[...] = curve_rows()
    pair_curve = curve_copy(0, curve_out, curve_pair, other_core)
    pair_curve.start()
    b, r = part(mine, side, place)
    total = grad[b, r]
    for k in range(1, chips):
        p = far(k)
        far_copy(p, p).wait_recv()
        total = total + far_in[p]
    final[b, r] = total
    for k in range(1, chips):
        all_copy(far(k), place).start()
    side_copy(side, place).start()
    fwd_copy(mine, side, place).start()
    pair_curve.wait_recv()
    curve_sum[...] = curve_out[...] + curve_pair[...]
    for k in range(1, peers):
        cpeer_copy(peer(k), chip).start()
    for k in range(1, chips):
        p = far(k)
        all_copy(p, p).wait_recv()
        side_copy(side, p).start()
        fwd_copy(mine, side, p).start()
    for k in range(chips):
        p = far(k)
        side_copy(1 - side, p).wait_recv()
        fwd_copy(mine, 1 - side, p).start()
    for p in range(peers):

        @pl.when(p != chip)
        def _():
            cpeer_copy(p, p).wait_recv()

        @pl.when(p == chip)
        def _():
            curve_peer[p] = curve_sum[...]

    curve = curve_peer[0]
    for p in range(1, peers):
        curve = curve + curve_peer[p]
    curve_half[...] = curve
    far_curve = curve_copy(1, curve_half, curve_far, other_grp)
    far_curve.start()
    for on in (side, 1 - side):
        for k in range(chips):
            fwd_copy(theirs, on, far(k)).wait_recv()
    sum_ref[...] = final[...]
    far_curve.wait_recv()
    curve_ref[...] = curve_half[...] + curve_far[...]

    far_curve.wait_send()
    pair_curve.wait_send()
    for j in range(blocks):
        pair_copy(j).wait_send()
    for j in range(own):
        near_copy(j).wait_send()
    for k in range(1, chips):
        far_copy(far(k), place).wait_send()
        all_copy(far(k), place).wait_send()
    for k in range(1, peers):
        cpeer_copy(peer(k), chip).wait_send()
    for k in range(chips):
        side_copy(side, far(k)).wait_send()
        fwd_copy(mine, side, far(k)).wait_send()
        fwd_copy(mine, 1 - side, far(k)).wait_send()


def finish(*refs):
    inputs, (res_out, step_w_ref, step_b_ref, step_o_ref, curve_ref), local, load_sem = (
        refs[:3],
        refs[3:8],
        refs[8:11],
        refs[11],
    )
    loads = [pltpu.make_async_copy(a, b, load_sem.at[i]) for i, (a, b) in enumerate(zip(inputs, local))]
    for load in loads:
        load.start()
    for load in loads:
        load.wait()
    res_ref, sum_ref, part_ref = local
    feats, _, hidden = step_w_ref.shape
    res_out[...] = res_ref[...]
    squares = jnp.zeros(sum_ref.shape[1:], f32)
    for j in range(hidden // LANES):
        squares = squares + sum_ref[j] * sum_ref[j]
    squares = jnp.sum(jnp.sum(squares, axis=0, keepdims=True), axis=1, keepdims=True)
    inverse = 1.0 / jnp.sqrt(squares / (hidden * feats + 2 * hidden) + norm_eps)
    for j in range(hidden // LANES):
        r = slice(j * LANES, (j + 1) * LANES)
        step = sum_ref[j] * inverse
        step_w_ref[:, 0, r] = step[:feats]
        step_b_ref[:, r] = step[feats : feats + 1]
        step_o_ref[:, r] = step[feats + 1 : feats + 2]
    curve = part_ref[0:2, 0:feats]
    mean = jnp.sum(jnp.sum(curve * curve, axis=0, keepdims=True), axis=1, keepdims=True) / (2 * feats)
    curve_ref[...] = curve / jnp.sqrt(mean + norm_eps)


def body(
    n_path,
    start_state,
    shocks,
    drift_rate,
    vol_curve,
    weight_in,
    bias_in,
    weight_out,
    default_date,
    netting_set,
    loss_given,
):
    feats, paths = start_state.shape
    hidden = weight_in.shape[1]
    peers = n_path // 2
    half = hidden // 2
    blocks = half // LANES
    own = blocks // 2
    chips = peers // 2
    reduce = n_path % 4 == 0 and chips >= own and chips % own == 0 and chips // own <= 4
    split_rows = 8 * (chips // own if reduce else 1)
    depth = -(-(feats + 2) // split_rows) * split_rows
    sums = (hidden // LANES, depth, LANES)
    wide_row = (LANES, paths)
    tile = (8, LANES)
    inputs = [
        start_state,
        shocks,
        drift_rate[None, :],
        vol_curve[None, :],
        jnp.transpose(weight_in, (2, 0, 1)),
        bias_in,
        weight_out,
        default_date[None, :],
        netting_set[None, :],
        loss_given[None, :],
    ]
    scratch = [pltpu.VMEM((feats, hidden) if a.ndim == 3 else a.shape, a.dtype) for a in inputs]
    scratch += [
        pltpu.SemaphoreType.DMA((len(inputs),)),
        pltpu.VMEM(wide_row, f32),
        pltpu.VMEM(wide_row, f32),
        pltpu.VMEM(wide_row, f32),
        pltpu.VMEM((LANES, hidden), f32),
        pltpu.VMEM((hidden, 3 * LANES), bf16),
        pltpu.VMEM((2 * LANES, hidden), bf16),
        pltpu.VMEM((hidden, LANES), f32),
        pltpu.VMEM((3 * LANES, 2 * paths), bf16),
        pltpu.VMEM((3 * paths, 2 * LANES), bf16),
        pltpu.VMEM((hidden, paths), f32),
        pltpu.VMEM((hidden, paths), f32),
        pltpu.VMEM((hidden, paths), bf16),
        pltpu.VMEM((hidden, paths), bf16),
        pltpu.VMEM(wide_row, f32),
        pltpu.VMEM(wide_row, f32),
        pltpu.VMEM(sums, f32),
        pltpu.VMEM((8, paths), f32),
        pltpu.VMEM((8, paths), f32),
        pltpu.SemaphoreType.DMA((1,)),
        pltpu.SemaphoreType.DMA((1,)),
    ]
    outs = [
        jax.ShapeDtypeStruct((1, paths), f32),
        jax.ShapeDtypeStruct(sums, f32),
        jax.ShapeDtypeStruct(tile, f32),
    ]
    if reduce:
        scratch += [
            pltpu.VMEM((blocks,) + sums[1:], f32),
            pltpu.VMEM((own,) + sums[1:], f32),
            pltpu.VMEM((chips, depth * own // chips, LANES), f32),
            pltpu.VMEM(sums, f32),
            pltpu.VMEM(tile, f32),
            pltpu.VMEM(tile, f32),
            pltpu.VMEM(tile, f32),
            pltpu.VMEM((peers,) + tile, f32),
            pltpu.VMEM(tile, f32),
            pltpu.VMEM(tile, f32),
        ]
        scratch += [pltpu.SemaphoreType.DMA((blocks,))] * 2
        scratch += [pltpu.SemaphoreType.DMA((own,))] * 2
        scratch += [pltpu.SemaphoreType.DMA((chips,))] * 4
        scratch += [pltpu.SemaphoreType.DMA((peers,))] * 2
        scratch += [pltpu.SemaphoreType.DMA((chips,))] * 2
        scratch += [pltpu.SemaphoreType.DMA((2,))] * 2
        scratch += [pltpu.SemaphoreType.DMA((peers,))] * 2
    vmem = pl.BlockSpec(memory_space=pltpu.VMEM)
    residual, total, curve = pl.pallas_call(
        functools.partial(kernel, n_path, reduce),
        out_shape=outs,
        in_specs=[pl.BlockSpec(memory_space=pltpu.HBM)] * len(inputs),
        out_specs=[vmem] * len(outs),
        scratch_shapes=scratch,
        compiler_params=pltpu.CompilerParams(
            collective_id=0, has_side_effects=True, vmem_limit_bytes=60 * 1024 * 1024
        ),
        name="bsde_step",
    )(*inputs)
    if not reduce:
        total = lax.psum(total, "path")
        curve = lax.psum(curve, ("grp", "path"))
    residual, step_w, step_b, step_o, curve_step = pl.pallas_call(
        finish,
        out_shape=[
            jax.ShapeDtypeStruct((1, paths), f32),
            jax.ShapeDtypeStruct((feats, 1, hidden), f32),
            jax.ShapeDtypeStruct((1, hidden), f32),
            jax.ShapeDtypeStruct((1, hidden), f32),
            jax.ShapeDtypeStruct((2, feats), f32),
        ],
        in_specs=[pl.BlockSpec(memory_space=pltpu.HBM)] * 3,
        out_specs=[vmem] * 5,
        scratch_shapes=[pltpu.VMEM(a.shape, f32) for a in (residual, total, curve)]
        + [pltpu.SemaphoreType.DMA((3,))],
        compiler_params=pltpu.CompilerParams(vmem_limit_bytes=60 * 1024 * 1024),
        name="normalize",
    )(residual, total, curve)
    return (residual, jnp.transpose(step_w, (1, 2, 0)), step_b, step_o, curve_step)


def solution(mesh):
    return jax.shard_map(
        functools.partial(body, mesh.shape["path"]),
        mesh=mesh,
        in_specs=(
            P(None, "path"),
            P(None, "path"),
            P(),
            P(),
            P("grp", None, None),
            P("grp", None),
            P("grp", None),
            P("path"),
            P("path"),
            P(),
        ),
        out_specs=(P("grp", "path"), P("grp", None, None), P("grp", None), P("grp", None), P()),
        check_vma=False,
    )
```

```python
import functools
import jax
import jax.numpy as jnp
from jax import lax
from jax.experimental import pallas as pl
from jax.experimental.pallas import tpu as pltpu
from jax.sharding import PartitionSpec as P

step_dt = 0.25
root_dt = 0.5
growth_factor = 1.0075
fund_spread = 0.5
norm_eps = 1e-06

f32 = jnp.float32
bf16 = jnp.bfloat16
LANES = 128
MESH = pl.DeviceIdType.MESH


def split(a):
    hi = a.astype(bf16)
    return hi, (a - hi.astype(f32)).astype(bf16)


def dot(a, b):
    return jnp.dot(a, b, preferred_element_type=f32)


def fold(a):
    return a[:, :LANES] + a[:, LANES:]


def wide(a, width):
    return jnp.concatenate([a] * (width // LANES), axis=1)


def kernel(
    n_path,
    reduce,
    *rest,
):
    inputs, rest = rest[:10], rest[10:]
    res_ref, sum_ref, curve_ref = rest[:3]
    local, load_sem, save_sem, rest = rest[3:13], rest[13], rest[14], rest[15:]
    start_ref, shock_ref, drift_ref, vol_ref, w_ref, bias_ref, outer_ref, date_ref, set_ref, given_ref = local
    (
        x0,
        x1,
        sh,
        wp,
        wcat,
        wt,
        ocol,
        xcat,
        bt,
        h0s,
        h1s,
        s_hi,
        s_lo,
        dsum,
        x1sum,
        grad,
        swap_out,
        swap_in,
        swap_send,
        swap_recv,
        *rest,
    ) = rest
    feats, paths = start_ref.shape
    hidden = w_ref.shape[1]
    grp = lax.axis_index("grp")
    here = lax.axis_index("path")
    core = lax.rem(here, 2)
    chip = lax.div(here, 2)
    peers = n_path // 2
    half = hidden // 2
    other_grp = (1 - grp, here)
    other_core = (grp, chip * 2 + 1 - core)

    def peer(k):
        return lax.rem(chip + k, peers)

    loads = [pltpu.make_async_copy(a.at[:, 0, :] if i == 4 else a, b, load_sem.at[i]) for i, (a, b) in enumerate(zip(inputs, local))]
    for load in loads:
        load.start()
    barrier = pltpu.get_barrier_semaphore()
    pl.semaphore_signal(barrier, inc=1, device_id=other_grp, device_id_type=MESH)
    if reduce:
        pl.semaphore_signal(barrier, inc=1, device_id=other_core, device_id_type=MESH)
        for k in range(1, peers):
            pl.semaphore_signal(barrier, inc=1, device_id=(grp, peer(k) * 2 + core), device_id_type=MESH)

    for load in loads[:4] + loads[5:]:
        load.wait()

    rows = lax.broadcasted_iota(jnp.int32, (LANES, paths), 0)
    x0[...] = jnp.where(rows == feats, f32(1.0), f32(0.0))
    x0[0:feats, :] = start_ref[...]
    sh[...] = jnp.zeros_like(sh)
    sh[0:feats, :] = shock_ref[...]
    square = lax.broadcasted_iota(jnp.int32, (LANES, LANES), 0)
    curve_in = jnp.zeros((LANES, LANES), f32)
    pad = jnp.zeros((1, LANES - feats), f32)
    curve_in = jnp.where(square == 0, jnp.concatenate([drift_ref[...], pad], axis=1), curve_in)
    curve_in = jnp.where(square == 1, jnp.concatenate([vol_ref[...], pad], axis=1), curve_in)
    curve_col = curve_in.T
    drift = curve_col[:, 0:1]
    vol = curve_col[:, 1:2]
    shocks = sh[...]
    now = x0[...]
    nxt = now + drift * step_dt + vol * root_dt * shocks
    x1[...] = nxt
    for i, a in enumerate((now, nxt)):
        hi, lo = split(a)
        cols = slice(i * paths, (i + 1) * paths)
        xcat[0:LANES, cols] = hi
        xcat[LANES : 2 * LANES, cols] = hi
        xcat[2 * LANES :, cols] = lo
    tail_row = feats // 8 * 8
    wp[tail_row:, :] = jnp.zeros((LANES - tail_row, hidden), f32)
    loads[4].wait()
    wp[0:feats, :] = w_ref[...]
    wp[feats : feats + 1, :] = bias_ref[...]
    wp[feats + 1 : feats + 2, :] = outer_ref[...]
    dsum[...] = jnp.zeros_like(dsum)
    x1sum[...] = jnp.zeros_like(x1sum)

    def forward(j, carry):
        v0, v1 = carry
        base = pl.multiple_of(j * 2 * LANES, 2 * LANES)
        for k in range(2):
            r = pl.ds(pl.multiple_of(base + k * LANES, LANES), LANES)
            w = wp[:, r]
            hi, lo = split(w)
            wt[0:LANES, r] = hi
            wt[LANES:, r] = lo
            w = w.T
            ocol[r, :] = jnp.broadcast_to(w[:, feats + 1 : feats + 2], (LANES, LANES))
            hi, lo = split(w)
            wcat[r, 0:LANES] = hi
            wcat[r, LANES : 2 * LANES] = lo
            wcat[r, 2 * LANES :] = hi
        r = pl.ds(base, 2 * LANES)
        z = dot(wcat[r, :], xcat[...])
        h0 = jnp.tanh(z[:, :paths])
        h1 = jnp.tanh(z[:, paths:])
        o = wide(ocol[r, :], paths)
        h0s[r, :] = h0
        h1s[r, :] = h1
        hi, lo = split(o * (1.0 - h0 * h0))
        s_hi[r, :] = hi
        s_lo[r, :] = lo
        d = dot(wt[:, r], hi)
        dsum[...] += d[:LANES] + d[LANES:] + dot(wt[0:LANES, r], lo)
        v0 = v0 + jnp.sum(o * h0, axis=0, keepdims=True)
        v1 = v1 + jnp.sum(o * h1, axis=0, keepdims=True)
        return v0, v1

    zero = jnp.zeros((1, paths), f32)
    v0, v1 = lax.fori_loop(0, hidden // (2 * LANES), forward, (zero, zero), unroll=4)
    inner = dsum[...]
    delta = vol * inner
    rest_own = -growth_factor * v0 - root_dt * jnp.sum(delta * shocks, axis=0, keepdims=True)
    square_own = jnp.sum(delta * delta, axis=0, keepdims=True)
    swap_out[0:1, :] = v1
    swap_out[1:2, :] = rest_own
    swap_out[2:3, :] = square_own
    swap_out[3:, :] = jnp.zeros((5, paths), f32)

    pl.semaphore_wait(barrier, peers + 1 if reduce else 1)
    swap = pltpu.make_async_remote_copy(
        src_ref=swap_out,
        dst_ref=swap_in,
        send_sem=swap_send.at[0],
        recv_sem=swap_recv.at[0],
        device_id=other_grp,
        device_id_type=MESH,
    )
    swap.start()
    for i, a in ((1, x0), (2, x1)):
        hi, lo = split(a[...].T)
        r = slice(i * paths, (i + 1) * paths)
        bt[r, 0:LANES] = hi
        bt[r, LANES:] = lo
    loss_row = zero
    for s in range(given_ref.shape[1]):
        loss_row = jnp.where(set_ref[...] == s, given_ref[0:1, s : s + 1], loss_row)
    defaulted = date_ref[...] == 1
    clean = jnp.full((1, paths), grp, jnp.int32) == 0
    swap.wait()

    got_v1, got_rest, got_square = swap_in[0:1, :], swap_in[1:2, :], swap_in[2:3, :]
    clean_v1 = jnp.where(clean, v1, got_v1)
    res_clean = clean_v1 + jnp.where(clean, rest_own, got_rest)
    margin = jnp.sqrt(jnp.where(clean, square_own, got_square) + norm_eps)
    tail = jnp.exp(-jnp.abs(clean_v1))
    softplus = jnp.maximum(clean_v1, 0.0) + jnp.log1p(tail)
    sigmoid = jnp.where(clean_v1 >= 0.0, f32(1.0), tail) / (1.0 + tail)
    target = jnp.where(defaulted, loss_row * softplus, jnp.where(clean, got_v1, v1))
    res_xva = target + jnp.where(clean, got_rest, rest_own) + step_dt * fund_spread * margin
    residual = jnp.where(clean, res_clean, res_xva)
    res_ref[...] = residual
    per = f32(1.0 / (n_path * paths))
    weighted = residual * per
    weighted_xva = res_xva * per
    cot_now = -growth_factor * weighted
    cot_next = jnp.where(
        clean,
        weighted + jnp.where(defaulted, loss_row * sigmoid * weighted_xva, f32(0.0)),
        jnp.where(defaulted, f32(0.0), weighted),
    )
    pull = jnp.where(clean, step_dt * fund_spread * weighted_xva / margin, f32(0.0))
    cot_delta = -root_dt * weighted * shocks + pull * delta
    cot_inner = vol * cot_delta
    hi, lo = split(cot_inner)
    xcat[0:LANES, 0:paths] = hi
    xcat[LANES : 2 * LANES, 0:paths] = hi
    xcat[2 * LANES :, 0:paths] = lo
    hi, lo = split(cot_inner.T)
    bt[0:paths, 0:LANES] = hi
    bt[0:paths, LANES:] = lo
    lane = lax.broadcasted_iota(jnp.int32, (2 * LANES, LANES), 1)

    def backward(b):
        r = pl.ds(pl.multiple_of(b * LANES, 2 * LANES), 2 * LANES)
        h0 = h0s[r, :]
        h1 = h1s[r, :]
        o = wide(ocol[r, :], paths)
        gap = 1.0 - h0 * h0
        t = dot(wcat[r, :], xcat[:, 0:paths])
        total = jnp.sum(t * gap + cot_now * h0 + cot_next * h1, axis=1, keepdims=True)
        y0_hi, y0_lo = split(o * gap * (cot_now - 2.0 * h0 * t))
        y1_hi, y1_lo = split(o * (1.0 - h1 * h1) * cot_next)
        a_hi = jnp.concatenate([s_hi[r, :], y0_hi, y1_hi], axis=1)
        a_lo = jnp.concatenate([s_lo[r, :], y0_lo, y1_lo], axis=1)
        g = fold(dot(a_hi, bt[...])) + dot(a_lo, bt[:, 0:LANES])
        g = g + jnp.where(lane == feats + 1, total, f32(0.0))
        depth = grad.shape[1]
        grad[b] = g[:LANES].T[:depth]
        grad[b + 1] = g[LANES:].T[:depth]
        back = dot(wt[:, r], y1_hi)
        x1sum[...] += back[:LANES] + back[LANES:] + dot(wt[0:LANES, r], y1_lo)

    def curve_rows():
        back = x1sum[...]
        by_drift = fold(step_dt * back).T
        by_vol = fold(root_dt * shocks * back + cot_delta * inner).T
        sub = lax.broadcasted_iota(jnp.int32, (8, LANES), 0)
        return jnp.where(
            sub == 0,
            jnp.sum(by_drift, axis=0, keepdims=True),
            jnp.where(sub == 1, jnp.sum(by_vol, axis=0, keepdims=True), f32(0.0)),
        )

    if not reduce:

        def whole_block(j, carry):
            backward(j * 2)
            return carry

        lax.fori_loop(0, hidden // (2 * LANES), whole_block, 0)
        save = pltpu.make_async_copy(grad, sum_ref, save_sem.at[0])
        save.start()
        save.wait()
        curve_ref[...] = curve_rows()
        return

    (
        pair_in,
        near_in,
        far_in,
        final,
        curve_out,
        curve_pair,
        curve_sum,
        curve_peer,
        curve_half,
        curve_far,
        pair_send,
        pair_recv,
        near_send,
        near_recv,
        far_send,
        far_recv,
        all_send,
        all_recv,
        fwd_send,
        fwd_recv,
        side_send,
        side_recv,
        curve_send,
        curve_recv,
        cpeer_send,
        cpeer_recv,
    ) = rest
    blocks = half // LANES
    own = blocks // 2
    chips = peers // 2
    per_block = chips // own
    chunk = grad.shape[1] // per_block
    side = lax.rem(chip, 2)
    place = lax.div(chip, 2)
    mine = core * blocks
    theirs = (1 - core) * blocks
    near = (grp, (place * 2 + 1 - side) * 2 + core)

    def far(k):
        return lax.rem(place + k, chips)

    def part(start, on, owner):
        return (
            start + on * own + lax.div(owner, per_block),
            pl.ds(pl.multiple_of(lax.rem(owner, per_block) * chunk, chunk), chunk),
        )

    def copy(src, dst, send, recv, to):
        return pltpu.make_async_remote_copy(
            src_ref=src, dst_ref=dst, send_sem=send, recv_sem=recv, device_id=to, device_id_type=MESH
        )

    def pair_copy(b):
        return copy(grad.at[theirs + b], pair_in.at[b], pair_send.at[b], pair_recv.at[b], other_core)

    def near_copy(i):
        block = mine + (1 - side) * own + i
        return copy(grad.at[block], near_in.at[i], near_send.at[i], near_recv.at[i], near)

    def far_copy(owner, slot):
        b, r = part(mine, side, owner)
        to = (grp, (owner * 2 + side) * 2 + core)
        return copy(grad.at[b, r], far_in.at[slot], far_send.at[owner], far_recv.at[slot], to)

    def all_copy(to, owner):
        b, r = part(mine, side, owner)
        to_device = (grp, (to * 2 + side) * 2 + core)
        return copy(final.at[b, r], final.at[b, r], all_send.at[to], all_recv.at[owner], to_device)

    def side_copy(on, owner):
        b, r = part(mine, on, owner)
        return copy(final.at[b, r], final.at[b, r], side_send.at[owner], side_recv.at[owner], near)

    def fwd_copy(start, on, owner):
        b, r = part(start, on, owner)
        i = on * chips + owner
        return copy(final.at[b, r], final.at[b, r], fwd_send.at[i], fwd_recv.at[i], other_core)

    def curve_copy(i, src, dst, to):
        return pltpu.make_async_remote_copy(
            src_ref=src,
            dst_ref=dst,
            send_sem=curve_send.at[i],
            recv_sem=curve_recv.at[i],
            device_id=to,
            device_id_type=MESH,
        )

    def cpeer_copy(to, slot):
        return pltpu.make_async_remote_copy(
            src_ref=curve_sum,
            dst_ref=curve_peer.at[slot],
            send_sem=cpeer_send.at[to],
            recv_sem=cpeer_recv.at[slot],
            device_id=(grp, to * 2 + core),
            device_id_type=MESH,
        )

    def their_blocks(j, carry):
        b = lax.rem((1 - side) * own + j * 2, blocks)
        backward(theirs + b)
        pair_copy(b).start()
        pair_copy(b + 1).start()
        return carry

    def near_blocks(j, carry):
        b = (1 - side) * own + j * 2
        backward(mine + b)
        for k in range(2):
            pair_copy(b + k).wait_recv()
            grad[mine + b + k] += pair_in[b + k]
            near_copy(j * 2 + k).start()
        return carry

    def my_blocks(j, carry):
        b = side * own + j * 2
        backward(mine + b)
        for k in range(2):
            pair_copy(b + k).wait_recv()
            near_copy(j * 2 + k).wait_recv()
            grad[mine + b + k] += pair_in[b + k] + near_in[j * 2 + k]
            for i in range(per_block):
                owner = (j * 2 + k) * per_block + i

                @pl.when(owner != place)
                def _():
                    far_copy(owner, place).start()

        return carry

    lax.fori_loop(0, blocks // 2, their_blocks, 0)
    lax.fori_loop(0, own // 2, near_blocks, 0)
    lax.fori_loop(0, own // 2, my_blocks, 0)
    curve_out[...] = curve_rows()
    pair_curve = curve_copy(0, curve_out, curve_pair, other_core)
    pair_curve.start()
    b, r = part(mine, side, place)
    total = grad[b, r]
    for k in range(1, chips):
        p = far(k)
        far_copy(p, p).wait_recv()
        total = total + far_in[p]
    final[b, r] = total
    for k in range(1, chips):
        all_copy(far(k), place).start()
    side_copy(side, place).start()
    fwd_copy(mine, side, place).start()
    pair_curve.wait_recv()
    curve_sum[...] = curve_out[...] + curve_pair[...]
    for k in range(1, peers):
        cpeer_copy(peer(k), chip).start()
    for k in range(1, chips):
        p = far(k)
        all_copy(p, p).wait_recv()
        side_copy(side, p).start()
        fwd_copy(mine, side, p).start()
    for k in range(chips):
        p = far(k)
        side_copy(1 - side, p).wait_recv()
        fwd_copy(mine, 1 - side, p).start()
    for p in range(peers):

        @pl.when(p != chip)
        def _():
            cpeer_copy(p, p).wait_recv()

        @pl.when(p == chip)
        def _():
            curve_peer[p] = curve_sum[...]

    curve = curve_peer[0]
    for p in range(1, peers):
        curve = curve + curve_peer[p]
    curve_half[...] = curve
    far_curve = curve_copy(1, curve_half, curve_far, other_grp)
    far_curve.start()
    saves = [
        pltpu.make_async_copy(final.at[pl.ds(h, blocks)], sum_ref.at[pl.ds(h, blocks)], save_sem.at[i])
        for i, h in enumerate((mine, theirs))
    ]
    saves[0].start()
    for on in (side, 1 - side):
        for k in range(chips):
            fwd_copy(theirs, on, far(k)).wait_recv()
    saves[1].start()
    far_curve.wait_recv()
    curve_ref[...] = curve_half[...] + curve_far[...]

    for save in saves:
        save.wait()
    far_curve.wait_send()
    pair_curve.wait_send()
    for j in range(blocks):
        pair_copy(j).wait_send()
    for j in range(own):
        near_copy(j).wait_send()
    for k in range(1, chips):
        far_copy(far(k), place).wait_send()
        all_copy(far(k), place).wait_send()
    for k in range(1, peers):
        cpeer_copy(peer(k), chip).wait_send()
    for k in range(chips):
        side_copy(side, far(k)).wait_send()
        fwd_copy(mine, side, far(k)).wait_send()
        fwd_copy(mine, 1 - side, far(k)).wait_send()


def finish(*refs):
    inputs, (res_out, step_w_ref, step_b_ref, step_o_ref, curve_ref), local, load_sem = (
        refs[:3],
        refs[3:8],
        refs[8:11],
        refs[11],
    )
    loads = [pltpu.make_async_copy(a, b, load_sem.at[i]) for i, (a, b) in enumerate(zip(inputs, local))]
    for load in loads:
        load.start()
    for load in loads:
        load.wait()
    res_ref, sum_ref, part_ref = local
    feats, _, hidden = step_w_ref.shape
    res_out[...] = res_ref[...]
    squares = jnp.zeros(sum_ref.shape[1:], f32)
    for j in range(hidden // LANES):
        squares = squares + sum_ref[j] * sum_ref[j]
    squares = jnp.sum(jnp.sum(squares, axis=0, keepdims=True), axis=1, keepdims=True)
    inverse = 1.0 / jnp.sqrt(squares / (hidden * feats + 2 * hidden) + norm_eps)
    for j in range(hidden // LANES):
        r = slice(j * LANES, (j + 1) * LANES)
        step = sum_ref[j] * inverse
        step_w_ref[:, 0, r] = step[:feats]
        step_b_ref[:, r] = step[feats : feats + 1]
        step_o_ref[:, r] = step[feats + 1 : feats + 2]
    curve = part_ref[0:2, 0:feats]
    mean = jnp.sum(jnp.sum(curve * curve, axis=0, keepdims=True), axis=1, keepdims=True) / (2 * feats)
    curve_ref[...] = curve / jnp.sqrt(mean + norm_eps)


def body(
    n_path,
    start_state,
    shocks,
    drift_rate,
    vol_curve,
    weight_in,
    bias_in,
    weight_out,
    default_date,
    netting_set,
    loss_given,
):
    feats, paths = start_state.shape
    hidden = weight_in.shape[1]
    peers = n_path // 2
    half = hidden // 2
    blocks = half // LANES
    own = blocks // 2
    chips = peers // 2
    reduce = n_path % 4 == 0 and chips >= own and chips % own == 0 and chips // own <= 4
    split_rows = 8 * (chips // own if reduce else 1)
    depth = -(-(feats + 2) // split_rows) * split_rows
    sums = (hidden // LANES, depth, LANES)
    wide_row = (LANES, paths)
    tile = (8, LANES)
    inputs = [
        start_state,
        shocks,
        drift_rate[None, :],
        vol_curve[None, :],
        jnp.transpose(weight_in, (2, 0, 1)),
        bias_in,
        weight_out,
        default_date[None, :],
        netting_set[None, :],
        loss_given[None, :],
    ]
    scratch = [pltpu.VMEM((feats, hidden) if a.ndim == 3 else a.shape, a.dtype) for a in inputs]
    scratch += [
        pltpu.SemaphoreType.DMA((len(inputs),)),
        pltpu.SemaphoreType.DMA((2,)),
        pltpu.VMEM(wide_row, f32),
        pltpu.VMEM(wide_row, f32),
        pltpu.VMEM(wide_row, f32),
        pltpu.VMEM((LANES, hidden), f32),
        pltpu.VMEM((hidden, 3 * LANES), bf16),
        pltpu.VMEM((2 * LANES, hidden), bf16),
        pltpu.VMEM((hidden, LANES), f32),
        pltpu.VMEM((3 * LANES, 2 * paths), bf16),
        pltpu.VMEM((3 * paths, 2 * LANES), bf16),
        pltpu.VMEM((hidden, paths), f32),
        pltpu.VMEM((hidden, paths), f32),
        pltpu.VMEM((hidden, paths), bf16),
        pltpu.VMEM((hidden, paths), bf16),
        pltpu.VMEM(wide_row, f32),
        pltpu.VMEM(wide_row, f32),
        pltpu.VMEM(sums, f32),
        pltpu.VMEM((8, paths), f32),
        pltpu.VMEM((8, paths), f32),
        pltpu.SemaphoreType.DMA((1,)),
        pltpu.SemaphoreType.DMA((1,)),
    ]
    outs = [
        jax.ShapeDtypeStruct((1, paths), f32),
        jax.ShapeDtypeStruct(sums, f32),
        jax.ShapeDtypeStruct(tile, f32),
    ]
    if reduce:
        scratch += [
            pltpu.VMEM((blocks,) + sums[1:], f32),
            pltpu.VMEM((own,) + sums[1:], f32),
            pltpu.VMEM((chips, depth * own // chips, LANES), f32),
            pltpu.VMEM(sums, f32),
            pltpu.VMEM(tile, f32),
            pltpu.VMEM(tile, f32),
            pltpu.VMEM(tile, f32),
            pltpu.VMEM((peers,) + tile, f32),
            pltpu.VMEM(tile, f32),
            pltpu.VMEM(tile, f32),
        ]
        scratch += [pltpu.SemaphoreType.DMA((blocks,))] * 2
        scratch += [pltpu.SemaphoreType.DMA((own,))] * 2
        scratch += [pltpu.SemaphoreType.DMA((chips,))] * 4
        scratch += [pltpu.SemaphoreType.DMA((peers,))] * 2
        scratch += [pltpu.SemaphoreType.DMA((chips,))] * 2
        scratch += [pltpu.SemaphoreType.DMA((2,))] * 2
        scratch += [pltpu.SemaphoreType.DMA((peers,))] * 2
    vmem = pl.BlockSpec(memory_space=pltpu.VMEM)
    residual, total, curve = pl.pallas_call(
        functools.partial(kernel, n_path, reduce),
        out_shape=outs,
        in_specs=[pl.BlockSpec(memory_space=pltpu.HBM)] * len(inputs),
        out_specs=[vmem, pl.BlockSpec(memory_space=pltpu.HBM), vmem],
        scratch_shapes=scratch,
        compiler_params=pltpu.CompilerParams(
            collective_id=0, has_side_effects=True, vmem_limit_bytes=60 * 1024 * 1024
        ),
        name="bsde_step",
    )(*inputs)
    if not reduce:
        total = lax.psum(total, "path")
        curve = lax.psum(curve, ("grp", "path"))
    residual, step_w, step_b, step_o, curve_step = pl.pallas_call(
        finish,
        out_shape=[
            jax.ShapeDtypeStruct((1, paths), f32),
            jax.ShapeDtypeStruct((feats, 1, hidden), f32),
            jax.ShapeDtypeStruct((1, hidden), f32),
            jax.ShapeDtypeStruct((1, hidden), f32),
            jax.ShapeDtypeStruct((2, feats), f32),
        ],
        in_specs=[pl.BlockSpec(memory_space=pltpu.HBM)] * 3,
        out_specs=[vmem] * 5,
        scratch_shapes=[pltpu.VMEM(a.shape, f32) for a in (residual, total, curve)]
        + [pltpu.SemaphoreType.DMA((3,))],
        compiler_params=pltpu.CompilerParams(vmem_limit_bytes=60 * 1024 * 1024),
        name="normalize",
    )(residual, total, curve)
    return (residual, jnp.transpose(step_w, (1, 2, 0)), step_b, step_o, curve_step)


def solution(mesh):
    return jax.shard_map(
        functools.partial(body, mesh.shape["path"]),
        mesh=mesh,
        in_specs=(
            P(None, "path"),
            P(None, "path"),
            P(),
            P(),
            P("grp", None, None),
            P("grp", None),
            P("grp", None),
            P("path"),
            P("path"),
            P(),
        ),
        out_specs=(P("grp", "path"), P("grp", None, None), P("grp", None), P("grp", None), P()),
        check_vma=False,
    )
```

```python
import functools
import jax
import jax.numpy as jnp
from jax import lax
from jax.experimental import pallas as pl
from jax.experimental.pallas import tpu as pltpu
from jax.sharding import PartitionSpec as P

step_dt = 0.25
root_dt = 0.5
growth_factor = 1.0075
fund_spread = 0.5
norm_eps = 1e-06

f32 = jnp.float32
bf16 = jnp.bfloat16
LANES = 128
MESH = pl.DeviceIdType.MESH


def split(a):
    hi = a.astype(bf16)
    return hi, (a - hi.astype(f32)).astype(bf16)


def dot(a, b):
    return jnp.dot(a, b, preferred_element_type=f32)


def fold(a):
    return a[:, :LANES] + a[:, LANES:]


def wide(a, width):
    return jnp.concatenate([a] * (width // LANES), axis=1)


def kernel(
    n_path,
    reduce,
    *rest,
):
    inputs, rest = rest[:10], rest[10:]
    res_ref, sum_ref, curve_ref = rest[:3]
    local, load_sem, save_sem, rest = rest[3:13], rest[13], rest[14], rest[15:]
    start_ref, shock_ref, drift_ref, vol_ref, w_ref, bias_ref, outer_ref, date_ref, set_ref, given_ref = local
    (
        x0,
        x1,
        sh,
        wp,
        wcat,
        wt,
        ocol,
        xcat,
        bt,
        h0s,
        h1s,
        s_hi,
        s_lo,
        dsum,
        x1sum,
        grad,
        swap_out,
        swap_in,
        swap_send,
        swap_recv,
        *rest,
    ) = rest
    feats, paths = start_ref.shape
    hidden = w_ref.shape[1]
    grp = lax.axis_index("grp")
    here = lax.axis_index("path")
    core = lax.rem(here, 2)
    chip = lax.div(here, 2)
    peers = n_path // 2
    half = hidden // 2
    other_grp = (1 - grp, here)
    other_core = (grp, chip * 2 + 1 - core)

    def peer(k):
        return lax.rem(chip + k, peers)

    loads = [pltpu.make_async_copy(a.at[:, 0, :] if i == 4 else a, b, load_sem.at[i]) for i, (a, b) in enumerate(zip(inputs, local))]
    for load in loads:
        load.start()
    barrier = pltpu.get_barrier_semaphore()
    pl.semaphore_signal(barrier, inc=1, device_id=other_grp, device_id_type=MESH)
    if reduce:
        pl.semaphore_signal(barrier, inc=1, device_id=other_core, device_id_type=MESH)
        for k in range(1, peers):
            pl.semaphore_signal(barrier, inc=1, device_id=(grp, peer(k) * 2 + core), device_id_type=MESH)

    for load in loads[:4] + loads[5:]:
        load.wait()

    rows = lax.broadcasted_iota(jnp.int32, (LANES, paths), 0)
    x0[...] = jnp.where(rows == feats, f32(1.0), f32(0.0))
    x0[0:feats, :] = start_ref[...]
    sh[...] = jnp.zeros_like(sh)
    sh[0:feats, :] = shock_ref[...]
    square = lax.broadcasted_iota(jnp.int32, (LANES, LANES), 0)
    curve_in = jnp.zeros((LANES, LANES), f32)
    pad = jnp.zeros((1, LANES - feats), f32)
    curve_in = jnp.where(square == 0, jnp.concatenate([drift_ref[...], pad], axis=1), curve_in)
    curve_in = jnp.where(square == 1, jnp.concatenate([vol_ref[...], pad], axis=1), curve_in)
    curve_col = curve_in.T
    drift = curve_col[:, 0:1]
    vol = curve_col[:, 1:2]
    shocks = sh[...]
    now = x0[...]
    nxt = now + drift * step_dt + vol * root_dt * shocks
    x1[...] = nxt
    for i, a in enumerate((now, nxt)):
        hi, lo = split(a)
        cols = slice(i * paths, (i + 1) * paths)
        xcat[0:LANES, cols] = hi
        xcat[LANES : 2 * LANES, cols] = hi
        xcat[2 * LANES :, cols] = lo
    tail_row = feats // 8 * 8
    wp[tail_row:, :] = jnp.zeros((LANES - tail_row, hidden), f32)
    loads[4].wait()
    wp[0:feats, :] = w_ref[...]
    wp[feats : feats + 1, :] = bias_ref[...]
    wp[feats + 1 : feats + 2, :] = outer_ref[...]
    dsum[...] = jnp.zeros_like(dsum)
    x1sum[...] = jnp.zeros_like(x1sum)

    def forward(j, carry):
        v0, v1 = carry
        base = pl.multiple_of(j * 2 * LANES, 2 * LANES)
        for k in range(2):
            r = pl.ds(pl.multiple_of(base + k * LANES, LANES), LANES)
            w = wp[:, r]
            hi, lo = split(w)
            wt[0:LANES, r] = hi
            wt[LANES:, r] = lo
            w = w.T
            ocol[r, :] = jnp.broadcast_to(w[:, feats + 1 : feats + 2], (LANES, LANES))
            hi, lo = split(w)
            wcat[r, 0:LANES] = hi
            wcat[r, LANES : 2 * LANES] = lo
            wcat[r, 2 * LANES :] = hi
        r = pl.ds(base, 2 * LANES)
        z = dot(wcat[r, :], xcat[...])
        h0 = jnp.tanh(z[:, :paths])
        h1 = jnp.tanh(z[:, paths:])
        o = wide(ocol[r, :], paths)
        h0s[r, :] = h0
        h1s[r, :] = h1
        hi, lo = split(o * (1.0 - h0 * h0))
        s_hi[r, :] = hi
        s_lo[r, :] = lo
        d = dot(wt[:, r], hi)
        dsum[...] += d[:LANES] + d[LANES:] + dot(wt[0:LANES, r], lo)
        v0 = v0 + jnp.sum(o * h0, axis=0, keepdims=True)
        v1 = v1 + jnp.sum(o * h1, axis=0, keepdims=True)
        return v0, v1

    zero = jnp.zeros((1, paths), f32)
    v0, v1 = lax.fori_loop(0, hidden // (2 * LANES), forward, (zero, zero))
    inner = dsum[...]
    delta = vol * inner
    rest_own = -growth_factor * v0 - root_dt * jnp.sum(delta * shocks, axis=0, keepdims=True)
    square_own = jnp.sum(delta * delta, axis=0, keepdims=True)
    swap_out[0:1, :] = v1
    swap_out[1:2, :] = rest_own
    swap_out[2:3, :] = square_own
    swap_out[3:, :] = jnp.zeros((5, paths), f32)

    pl.semaphore_wait(barrier, peers + 1 if reduce else 1)
    swap = pltpu.make_async_remote_copy(
        src_ref=swap_out,
        dst_ref=swap_in,
        send_sem=swap_send.at[0],
        recv_sem=swap_recv.at[0],
        device_id=other_grp,
        device_id_type=MESH,
    )
    swap.start()
    for i, a in ((1, x0), (2, x1)):
        hi, lo = split(a[...].T)
        r = slice(i * paths, (i + 1) * paths)
        bt[r, 0:LANES] = hi
        bt[r, LANES:] = lo
    loss_row = zero
    for s in range(given_ref.shape[1]):
        loss_row = jnp.where(set_ref[...] == s, given_ref[0:1, s : s + 1], loss_row)
    defaulted = date_ref[...] == 1
    clean = jnp.full((1, paths), grp, jnp.int32) == 0
    swap.wait()

    got_v1, got_rest, got_square = swap_in[0:1, :], swap_in[1:2, :], swap_in[2:3, :]
    clean_v1 = jnp.where(clean, v1, got_v1)
    res_clean = clean_v1 + jnp.where(clean, rest_own, got_rest)
    margin = jnp.sqrt(jnp.where(clean, square_own, got_square) + norm_eps)
    tail = jnp.exp(-jnp.abs(clean_v1))
    softplus = jnp.maximum(clean_v1, 0.0) + jnp.log1p(tail)
    sigmoid = jnp.where(clean_v1 >= 0.0, f32(1.0), tail) / (1.0 + tail)
    target = jnp.where(defaulted, loss_row * softplus, jnp.where(clean, got_v1, v1))
    res_xva = target + jnp.where(clean, got_rest, rest_own) + step_dt * fund_spread * margin
    residual = jnp.where(clean, res_clean, res_xva)
    res_ref[...] = residual
    per = f32(1.0 / (n_path * paths))
    weighted = residual * per
    weighted_xva = res_xva * per
    cot_now = -growth_factor * weighted
    cot_next = jnp.where(
        clean,
        weighted + jnp.where(defaulted, loss_row * sigmoid * weighted_xva, f32(0.0)),
        jnp.where(defaulted, f32(0.0), weighted),
    )
    pull = jnp.where(clean, step_dt * fund_spread * weighted_xva / margin, f32(0.0))
    cot_delta = -root_dt * weighted * shocks + pull * delta
    cot_inner = vol * cot_delta
    hi, lo = split(cot_inner)
    xcat[0:LANES, 0:paths] = hi
    xcat[LANES : 2 * LANES, 0:paths] = hi
    xcat[2 * LANES :, 0:paths] = lo
    hi, lo = split(cot_inner.T)
    bt[0:paths, 0:LANES] = hi
    bt[0:paths, LANES:] = lo
    lane = lax.broadcasted_iota(jnp.int32, (2 * LANES, LANES), 1)

    def backward(b):
        r = pl.ds(pl.multiple_of(b * LANES, 2 * LANES), 2 * LANES)
        h0 = h0s[r, :]
        h1 = h1s[r, :]
        o = wide(ocol[r, :], paths)
        gap = 1.0 - h0 * h0
        t = dot(wcat[r, :], xcat[:, 0:paths])
        total = jnp.sum(t * gap + cot_now * h0 + cot_next * h1, axis=1, keepdims=True)
        y0_hi, y0_lo = split(o * gap * (cot_now - 2.0 * h0 * t))
        y1_hi, y1_lo = split(o * (1.0 - h1 * h1) * cot_next)
        a_hi = jnp.concatenate([s_hi[r, :], y0_hi, y1_hi], axis=1)
        a_lo = jnp.concatenate([s_lo[r, :], y0_lo, y1_lo], axis=1)
        g = fold(dot(a_hi, bt[...])) + dot(a_lo, bt[:, 0:LANES])
        g = g + jnp.where(lane == feats + 1, total, f32(0.0))
        depth = grad.shape[1]
        grad[b] = g[:LANES].T[:depth]
        grad[b + 1] = g[LANES:].T[:depth]
        back = dot(wt[:, r], y1_hi)
        x1sum[...] += back[:LANES] + back[LANES:] + dot(wt[0:LANES, r], y1_lo)

    def curve_rows():
        back = x1sum[...]
        by_drift = fold(step_dt * back).T
        by_vol = fold(root_dt * shocks * back + cot_delta * inner).T
        sub = lax.broadcasted_iota(jnp.int32, (8, LANES), 0)
        return jnp.where(
            sub == 0,
            jnp.sum(by_drift, axis=0, keepdims=True),
            jnp.where(sub == 1, jnp.sum(by_vol, axis=0, keepdims=True), f32(0.0)),
        )

    if not reduce:

        def whole_block(j, carry):
            backward(j * 2)
            return carry

        lax.fori_loop(0, hidden // (2 * LANES), whole_block, 0)
        save = pltpu.make_async_copy(grad, sum_ref, save_sem.at[0])
        save.start()
        save.wait()
        curve_ref[...] = curve_rows()
        return

    (
        pair_in,
        near_in,
        far_in,
        final,
        curve_out,
        curve_pair,
        curve_sum,
        curve_peer,
        curve_half,
        curve_far,
        pair_send,
        pair_recv,
        near_send,
        near_recv,
        far_send,
        far_recv,
        all_send,
        all_recv,
        fwd_send,
        fwd_recv,
        side_send,
        side_recv,
        curve_send,
        curve_recv,
        cpeer_send,
        cpeer_recv,
    ) = rest
    blocks = half // LANES
    own = blocks // 2
    chips = peers // 2
    per_block = chips // own
    chunk = grad.shape[1] // per_block
    side = lax.rem(chip, 2)
    place = lax.div(chip, 2)
    mine = core * blocks
    theirs = (1 - core) * blocks
    near = (grp, (place * 2 + 1 - side) * 2 + core)

    def far(k):
        return lax.rem(place + k, chips)

    def part(start, on, owner):
        return (
            start + on * own + lax.div(owner, per_block),
            pl.ds(pl.multiple_of(lax.rem(owner, per_block) * chunk, chunk), chunk),
        )

    def copy(src, dst, send, recv, to):
        return pltpu.make_async_remote_copy(
            src_ref=src, dst_ref=dst, send_sem=send, recv_sem=recv, device_id=to, device_id_type=MESH
        )

    def pair_copy(b):
        return copy(grad.at[theirs + b], pair_in.at[b], pair_send.at[b], pair_recv.at[b], other_core)

    def near_copy(i):
        block = mine + (1 - side) * own + i
        return copy(grad.at[block], near_in.at[i], near_send.at[i], near_recv.at[i], near)

    def far_copy(owner, slot):
        b, r = part(mine, side, owner)
        to = (grp, (owner * 2 + side) * 2 + core)
        return copy(grad.at[b, r], far_in.at[slot], far_send.at[owner], far_recv.at[slot], to)

    def all_copy(to, owner):
        b, r = part(mine, side, owner)
        to_device = (grp, (to * 2 + side) * 2 + core)
        return copy(final.at[b, r], final.at[b, r], all_send.at[to], all_recv.at[owner], to_device)

    def side_copy(on, owner):
        b, r = part(mine, on, owner)
        return copy(final.at[b, r], final.at[b, r], side_send.at[owner], side_recv.at[owner], near)

    def fwd_copy(start, on, owner):
        b, r = part(start, on, owner)
        i = on * chips + owner
        return copy(final.at[b, r], final.at[b, r], fwd_send.at[i], fwd_recv.at[i], other_core)

    def curve_copy(i, src, dst, to):
        return pltpu.make_async_remote_copy(
            src_ref=src,
            dst_ref=dst,
            send_sem=curve_send.at[i],
            recv_sem=curve_recv.at[i],
            device_id=to,
            device_id_type=MESH,
        )

    def cpeer_copy(to, slot):
        return pltpu.make_async_remote_copy(
            src_ref=curve_sum,
            dst_ref=curve_peer.at[slot],
            send_sem=cpeer_send.at[to],
            recv_sem=cpeer_recv.at[slot],
            device_id=(grp, to * 2 + core),
            device_id_type=MESH,
        )

    def their_blocks(j, carry):
        b = lax.rem((1 - side) * own + j * 2, blocks)
        backward(theirs + b)
        pair_copy(b).start()
        pair_copy(b + 1).start()
        return carry

    def near_blocks(j, carry):
        b = (1 - side) * own + j * 2
        backward(mine + b)
        for k in range(2):
            pair_copy(b + k).wait_recv()
            grad[mine + b + k] += pair_in[b + k]
            near_copy(j * 2 + k).start()
        return carry

    def my_blocks(j, carry):
        b = side * own + j * 2
        backward(mine + b)
        for k in range(2):
            pair_copy(b + k).wait_recv()
            near_copy(j * 2 + k).wait_recv()
            grad[mine + b + k] += pair_in[b + k] + near_in[j * 2 + k]
            for i in range(per_block):
                owner = (j * 2 + k) * per_block + i

                @pl.when(owner != place)
                def _():
                    far_copy(owner, place).start()

        return carry

    lax.fori_loop(0, blocks // 2, their_blocks, 0)
    lax.fori_loop(0, own // 2, near_blocks, 0)
    lax.fori_loop(0, own // 2, my_blocks, 0)
    curve_out[...] = curve_rows()
    pair_curve = curve_copy(0, curve_out, curve_pair, other_core)
    pair_curve.start()
    b, r = part(mine, side, place)
    total = grad[b, r]
    for k in range(1, chips):
        p = far(k)
        far_copy(p, p).wait_recv()
        total = total + far_in[p]
    final[b, r] = total
    for k in range(1, chips):
        all_copy(far(k), place).start()
    side_copy(side, place).start()
    fwd_copy(mine, side, place).start()
    pair_curve.wait_recv()
    curve_sum[...] = curve_out[...] + curve_pair[...]
    for k in range(1, peers):
        cpeer_copy(peer(k), chip).start()
    for k in range(1, chips):
        p = far(k)
        all_copy(p, p).wait_recv()
        side_copy(side, p).start()
        fwd_copy(mine, side, p).start()
    for k in range(chips):
        p = far(k)
        side_copy(1 - side, p).wait_recv()
        fwd_copy(mine, 1 - side, p).start()
    for p in range(peers):

        @pl.when(p != chip)
        def _():
            cpeer_copy(p, p).wait_recv()

        @pl.when(p == chip)
        def _():
            curve_peer[p] = curve_sum[...]

    curve = curve_peer[0]
    for p in range(1, peers):
        curve = curve + curve_peer[p]
    curve_half[...] = curve
    far_curve = curve_copy(1, curve_half, curve_far, other_grp)
    far_curve.start()
    saves = [
        pltpu.make_async_copy(final.at[pl.ds(h, blocks)], sum_ref.at[pl.ds(h, blocks)], save_sem.at[i])
        for i, h in enumerate((mine, theirs))
    ]
    saves[0].start()
    for on in (side, 1 - side):
        for k in range(chips):
            fwd_copy(theirs, on, far(k)).wait_recv()
    saves[1].start()
    far_curve.wait_recv()
    curve_ref[...] = curve_half[...] + curve_far[...]

    for save in saves:
        save.wait()
    far_curve.wait_send()
    pair_curve.wait_send()
    for j in range(blocks):
        pair_copy(j).wait_send()
    for j in range(own):
        near_copy(j).wait_send()
    for k in range(1, chips):
        far_copy(far(k), place).wait_send()
        all_copy(far(k), place).wait_send()
    for k in range(1, peers):
        cpeer_copy(peer(k), chip).wait_send()
    for k in range(chips):
        side_copy(side, far(k)).wait_send()
        fwd_copy(mine, side, far(k)).wait_send()
        fwd_copy(mine, 1 - side, far(k)).wait_send()


def finish(*refs):
    inputs, (res_out, step_w_ref, step_b_ref, step_o_ref, curve_ref), local, load_sem = (
        refs[:3],
        refs[3:8],
        refs[8:11],
        refs[11],
    )
    loads = [pltpu.make_async_copy(a, b, load_sem.at[i]) for i, (a, b) in enumerate(zip(inputs, local))]
    for load in loads:
        load.start()
    for load in loads:
        load.wait()
    res_ref, sum_ref, part_ref = local
    feats, _, hidden = step_w_ref.shape
    res_out[...] = res_ref[...]
    squares = jnp.zeros(sum_ref.shape[1:], f32)
    for j in range(hidden // LANES):
        squares = squares + sum_ref[j] * sum_ref[j]
    squares = jnp.sum(jnp.sum(squares, axis=0, keepdims=True), axis=1, keepdims=True)
    inverse = 1.0 / jnp.sqrt(squares / (hidden * feats + 2 * hidden) + norm_eps)
    for j in range(hidden // LANES):
        r = slice(j * LANES, (j + 1) * LANES)
        step = sum_ref[j] * inverse
        step_w_ref[:, 0, r] = step[:feats]
        step_b_ref[:, r] = step[feats : feats + 1]
        step_o_ref[:, r] = step[feats + 1 : feats + 2]
    curve = part_ref[0:2, 0:feats]
    mean = jnp.sum(jnp.sum(curve * curve, axis=0, keepdims=True), axis=1, keepdims=True) / (2 * feats)
    curve_ref[...] = curve / jnp.sqrt(mean + norm_eps)


def body(
    n_path,
    start_state,
    shocks,
    drift_rate,
    vol_curve,
    weight_in,
    bias_in,
    weight_out,
    default_date,
    netting_set,
    loss_given,
):
    feats, paths = start_state.shape
    hidden = weight_in.shape[1]
    peers = n_path // 2
    half = hidden // 2
    blocks = half // LANES
    own = blocks // 2
    chips = peers // 2
    reduce = n_path % 4 == 0 and chips >= own and chips % own == 0 and chips // own <= 4
    split_rows = 8 * (chips // own if reduce else 1)
    depth = -(-(feats + 2) // split_rows) * split_rows
    sums = (hidden // LANES, depth, LANES)
    wide_row = (LANES, paths)
    tile = (8, LANES)
    inputs = [
        start_state,
        shocks,
        drift_rate[None, :],
        vol_curve[None, :],
        jnp.transpose(weight_in, (2, 0, 1)),
        bias_in,
        weight_out,
        default_date[None, :],
        netting_set[None, :],
        loss_given[None, :],
    ]
    scratch = [pltpu.VMEM((feats, hidden) if a.ndim == 3 else a.shape, a.dtype) for a in inputs]
    scratch += [
        pltpu.SemaphoreType.DMA((len(inputs),)),
        pltpu.SemaphoreType.DMA((2,)),
        pltpu.VMEM(wide_row, f32),
        pltpu.VMEM(wide_row, f32),
        pltpu.VMEM(wide_row, f32),
        pltpu.VMEM((LANES, hidden), f32),
        pltpu.VMEM((hidden, 3 * LANES), bf16),
        pltpu.VMEM((2 * LANES, hidden), bf16),
        pltpu.VMEM((hidden, LANES), f32),
        pltpu.VMEM((3 * LANES, 2 * paths), bf16),
        pltpu.VMEM((3 * paths, 2 * LANES), bf16),
        pltpu.VMEM((hidden, paths), f32),
        pltpu.VMEM((hidden, paths), f32),
        pltpu.VMEM((hidden, paths), bf16),
        pltpu.VMEM((hidden, paths), bf16),
        pltpu.VMEM(wide_row, f32),
        pltpu.VMEM(wide_row, f32),
        pltpu.VMEM(sums, f32),
        pltpu.VMEM((8, paths), f32),
        pltpu.VMEM((8, paths), f32),
        pltpu.SemaphoreType.DMA((1,)),
        pltpu.SemaphoreType.DMA((1,)),
    ]
    outs = [
        jax.ShapeDtypeStruct((1, paths), f32),
        jax.ShapeDtypeStruct(sums, f32),
        jax.ShapeDtypeStruct(tile, f32),
    ]
    if reduce:
        scratch += [
            pltpu.VMEM((blocks,) + sums[1:], f32),
            pltpu.VMEM((own,) + sums[1:], f32),
            pltpu.VMEM((chips, depth * own // chips, LANES), f32),
            pltpu.VMEM(sums, f32),
            pltpu.VMEM(tile, f32),
            pltpu.VMEM(tile, f32),
            pltpu.VMEM(tile, f32),
            pltpu.VMEM((peers,) + tile, f32),
            pltpu.VMEM(tile, f32),
            pltpu.VMEM(tile, f32),
        ]
        scratch += [pltpu.SemaphoreType.DMA((blocks,))] * 2
        scratch += [pltpu.SemaphoreType.DMA((own,))] * 2
        scratch += [pltpu.SemaphoreType.DMA((chips,))] * 4
        scratch += [pltpu.SemaphoreType.DMA((peers,))] * 2
        scratch += [pltpu.SemaphoreType.DMA((chips,))] * 2
        scratch += [pltpu.SemaphoreType.DMA((2,))] * 2
        scratch += [pltpu.SemaphoreType.DMA((peers,))] * 2
    vmem = pl.BlockSpec(memory_space=pltpu.VMEM)
    residual, total, curve = pl.pallas_call(
        functools.partial(kernel, n_path, reduce),
        out_shape=outs,
        in_specs=[pl.BlockSpec(memory_space=pltpu.HBM)] * len(inputs),
        out_specs=[vmem, pl.BlockSpec(memory_space=pltpu.HBM), vmem],
        scratch_shapes=scratch,
        compiler_params=pltpu.CompilerParams(
            collective_id=0, has_side_effects=True, vmem_limit_bytes=60 * 1024 * 1024
        ),
        name="bsde_step",
    )(*inputs)
    if not reduce:
        total = lax.psum(total, "path")
        curve = lax.psum(curve, ("grp", "path"))
    residual, step_w, step_b, step_o, curve_step = pl.pallas_call(
        finish,
        out_shape=[
            jax.ShapeDtypeStruct((1, paths), f32),
            jax.ShapeDtypeStruct((feats, 1, hidden), f32),
            jax.ShapeDtypeStruct((1, hidden), f32),
            jax.ShapeDtypeStruct((1, hidden), f32),
            jax.ShapeDtypeStruct((2, feats), f32),
        ],
        in_specs=[pl.BlockSpec(memory_space=pltpu.HBM)] * 3,
        out_specs=[vmem] * 5,
        scratch_shapes=[pltpu.VMEM(a.shape, f32) for a in (residual, total, curve)]
        + [pltpu.SemaphoreType.DMA((3,))],
        compiler_params=pltpu.CompilerParams(vmem_limit_bytes=60 * 1024 * 1024),
        name="normalize",
    )(residual, total, curve)
    return (residual, jnp.transpose(step_w, (1, 2, 0)), step_b, step_o, curve_step)


def solution(mesh):
    return jax.shard_map(
        functools.partial(body, mesh.shape["path"]),
        mesh=mesh,
        in_specs=(
            P(None, "path"),
            P(None, "path"),
            P(),
            P(),
            P("grp", None, None),
            P("grp", None),
            P("grp", None),
            P("path"),
            P("path"),
            P(),
        ),
        out_specs=(P("grp", "path"), P("grp", None, None), P("grp", None), P("grp", None), P()),
        check_vma=False,
    )
```
